32 devices in a mesh: grp: 8 (over z, core), tp: 4 (over y, x).
Axes of the slice: x: 2, y: 2, z: 4, core: 2. Of those that a mesh axis runs over, the one named last changes fastest.
Arguments:
- tokens: bfloat16 [8192, 8192], P(('grp', 'tp')), may hold values from -6 to 6
- frozen_weight: bfloat16 [8192, 10240], P(None, 'tp'), may hold values from -0.0625 to 0.0625
- down_weight: bfloat16 [32, 64, 8192], P('grp', None, 'tp'), may hold values from -0.0625 to 0.0625
- up_weight: bfloat16 [32, 64, 10240], P('grp', None, 'tp'), may hold values from -0.75 to 0.75
- adapter_storage_slot: int32 [32], replicated, may hold values from 0 to 31, as said below
- adapter_of_block: int32 [64], replicated, may hold values from 0 to 31, as said below
Outputs:
- qkv: bfloat16 [8192, 10240], P('grp', 'tp')
The draws below stay inside these ranges and needn't reach their ends.
Inputs may be any that keep to these rules, and one draw needn't show every extreme that they name: `adapter_storage_slot`: each slot is named by exactly one adapter; an adapter with slot s is stored by group s // 4. `adapter_of_block`: the 8 blocks of one group, blocks g * 8 to (g + 1) * 8 - 1, name adapters stored by 8 different groups.
All inputs are finite; a program needn't handle non-finite values.
Results may differ from the reference program's by a relative error of at most 0.0029.
Values may be sent and summed in bfloat16 or wider, within the bound.
No kernel may reach another device: no remote copies, remote signals or barrier semaphores. Data moves between devices by JAX's collectives and lax.ppermute only.
A program may use at most 128 MiB of HBM per device.

```python
import jax
import jax.numpy as jnp
from jax import lax

MODEL_WIDTH = 8192
ADAPTER_RANK = 64
BLOCK = 128
BLK_GRP = 8
ADP_GRP = 4
QUERY_KEY_VALUE = 10240
ADAPTER_COUNT = 32
BLOCKS = 64
ROWS = 8192


def adapter_plan(key):
    groups = BLOCKS // BLK_GRP
    slot_of = jax.random.permutation(jax.random.fold_in(key, 11), ADAPTER_COUNT).astype(jnp.int32)
    adapter_at = jnp.argsort(slot_of, stable=True).astype(jnp.int32)
    popular = jax.random.permutation(jax.random.fold_in(key, 12), groups).astype(jnp.int32)
    random_part = jax.random.randint(jax.random.fold_in(key, 13), (groups, groups), 0, groups)
    owner_score = (random_part + 2 * popular[None, :]) * groups + jnp.arange(groups, dtype=jnp.int32)[None, :]
    owner_pick = lax.top_k(owner_score, BLK_GRP)[1].astype(jnp.int32)
    local_slot = jax.random.randint(jax.random.fold_in(key, 14), (groups, BLK_GRP), 0, ADP_GRP)
    chosen = jnp.take(adapter_at, (owner_pick * ADP_GRP + local_slot).reshape(-1), axis=0)
    return (slot_of, chosen.astype(jnp.int32))


def draw_adapter_storage_slot(key, part):
    return adapter_plan(key)[0]


def draw_adapter_of_block(key, part):
    return adapter_plan(key)[1]


def shard_levels(own_key, dims, split, smallest, high):
    level, own = 1.0, jax.random.fold_in(own_key, 6)
    for position, parts in split:
        heights = jnp.exp(jax.random.uniform(jax.random.fold_in(own, position), (parts,), jnp.float32, smallest / len(split), high / len(split)))
        level = level * jnp.repeat(heights, dims[position] // parts).reshape([-1 if axis == position else 1 for axis in range(len(dims))])
    return level


def gaussian(stream_key, shape, scale, most, shards=(), held_as=jnp.bfloat16):
    result = jax.random.normal(stream_key, shape, jnp.float32) * scale
    if len(shards) > 0:
        result = shard_levels(stream_key, shape, shards, -0.22, 0.18) * result
    return jnp.clip(result, min=-most, max=most).astype(held_as)


def setup_inputs(seed: int = 0) -> dict:
    streams_of = jax.random.split(jax.random.key(seed), 7)
    tokens = gaussian(streams_of[0], (ROWS, MODEL_WIDTH), 1.0, 6.0, ((0, 32),))
    frozen_weight = gaussian(streams_of[1], (MODEL_WIDTH, QUERY_KEY_VALUE), MODEL_WIDTH ** -0.5, 0.0625, ((1, 4),))
    down_weight = gaussian(streams_of[2], (ADAPTER_COUNT, ADAPTER_RANK, MODEL_WIDTH), MODEL_WIDTH ** -0.5, 0.0625, ((0, 8), (2, 4)))
    up_weight = gaussian(streams_of[3], (ADAPTER_COUNT, ADAPTER_RANK, QUERY_KEY_VALUE), ADAPTER_RANK ** -0.5, 0.75, ((0, 8), (2, 4)))
    adapter_storage_slot = draw_adapter_storage_slot(jax.random.fold_in(streams_of[6], 71), 0)
    adapter_of_block = draw_adapter_of_block(jax.random.fold_in(streams_of[6], 71), 0)
    return {"tokens": tokens, "frozen_weight": frozen_weight, "down_weight": down_weight, "up_weight": up_weight, "adapter_storage_slot": adapter_storage_slot, "adapter_of_block": adapter_of_block}


adapter_scale = 0.5


def reference(tokens, frozen_weight, down_weight, up_weight, adapter_storage_slot, adapter_of_block):
    frozen_rows = jnp.dot(tokens, frozen_weight, preferred_element_type=jnp.float32)
    slot_numbers = jnp.take(adapter_storage_slot, adapter_of_block, axis=0).astype(jnp.int32)
    down_tile = jnp.take(down_weight, slot_numbers, axis=0).astype(jnp.float32)
    up_tile = jnp.take(up_weight, slot_numbers, axis=0).astype(jnp.float32)
    blocks = tokens.reshape(-1, BLOCK, MODEL_WIDTH).astype(jnp.float32)
    shrink = jnp.einsum("bnd,brd->bnr", blocks, down_tile).astype(jnp.bfloat16)
    update_rows = jnp.einsum("bnr,brc->bnc", shrink.astype(jnp.float32), up_tile)
    return (frozen_rows + adapter_scale * update_rows.reshape(frozen_rows.shape)).astype(jnp.bfloat16)
```

```python
import functools

import jax
import jax.numpy as jnp
from jax import lax
from jax.experimental import pallas as pl
from jax.experimental.pallas import tpu as pltpu
from jax.sharding import PartitionSpec as P

BLOCK = 128
MIB = 1 << 20

adapter_scale = 0.5


def tile_of(columns, most):
    return max(t for t in range(128, most + 1, 128) if columns % t == 0)


def pick_kernel(index_ref, source_ref, out_ref):
    out_ref[...] = source_ref[...]


def pick(source, index):
    count, block = index.shape[0], (1,) + source.shape[1:]
    return pl.pallas_call(
        pick_kernel,
        grid_spec=pltpu.PrefetchScalarGridSpec(
            num_scalar_prefetch=1,
            grid=(count,),
            in_specs=[pl.BlockSpec(block, lambda i, index: (index[i], 0, 0))],
            out_specs=pl.BlockSpec(block, lambda i, index: (i, 0, 0)),
        ),
        out_shape=jax.ShapeDtypeStruct((count,) + source.shape[1:], source.dtype),
        cost_estimate=pl.CostEstimate(
            flops=0, bytes_accessed=2 * count * source[0].size * 2, transcendentals=0
        ),
        name="pick_panels",
    )(index, source)


class Piece:
    def __init__(self, array, at=None):
        self.array, self.at = array, at

    def value(self):
        return self.array if self.at is None else self.array[self.at]


def gather_refs(pieces):
    arrays = []
    places = []
    for piece in pieces:
        for number, array in enumerate(arrays):
            if array is piece.array:
                break
        else:
            number = len(arrays)
            arrays.append(piece.array)
        places.append((number, piece.at))
    return arrays, places


def read(refs, place):
    number, at = place
    return refs[number][...] if at is None else refs[number][at]


def whole_spec(array):
    zeros = (0,) * array.ndim
    return pl.BlockSpec(array.shape, lambda n, *_: zeros)


def project_kernel(places, slices, with_total, order_ref, owner_ref, *refs):
    refs = list(refs)
    arrays = refs[: places["arrays"]]
    weights = refs[places["arrays"] : places["arrays"] + slices]
    rest = refs[places["arrays"] + slices :]
    half = weights[0].shape[0] // 2
    rows = places["rows"]
    out_ref = rest[-1]
    for number, pairs in enumerate(rows):
        total = None
        for weight, (first, second) in zip(weights, pairs):
            part = jnp.dot(read(arrays, first), weight[:half], preferred_element_type=jnp.float32)
            part += jnp.dot(read(arrays, second), weight[half:], preferred_element_type=jnp.float32)
            total = part if total is None else total + part
        if with_total:
            total_ref, shrink_ref, *panels = rest[:-2]
            total += total_ref[...]
            for block, panel in enumerate(panels):
                update = jnp.dot(
                    shrink_ref[:, block * panel.shape[1] : (block + 1) * panel.shape[1]],
                    panel[0],
                    preferred_element_type=jnp.float32,
                )
                span = pl.ds(block * BLOCK, BLOCK)
                out_ref[span, :] = (
                    total[block * BLOCK : (block + 1) * BLOCK] + adapter_scale * update
                ).astype(out_ref.dtype)
        else:
            out_ref[number] = total


def project(rows, order, weight, tile, total=None, shrink=None, panels=None, owner=None, out=None, name=None):
    flat = [piece for pairs in rows for pair in pairs for piece in pair]
    arrays, places = gather_refs(flat)
    slices = len(rows[0])
    grid_places, position = [], 0
    for pairs in rows:
        grid_places.append([(places[position + 2 * i], places[position + 2 * i + 1]) for i in range(len(pairs))])
        position += 2 * len(pairs)
    row_count, half = arrays[0].shape[-2:]
    columns = weight.shape[1]
    width = 2 * half
    in_specs = [whole_spec(a) for a in arrays]
    operands = list(arrays)
    for i in range(slices):
        in_specs.append(pl.BlockSpec((width, tile), lambda n, order, owner, i=i: (order[i], n)))
        operands.append(weight)
    aliases = {}
    if total is None:
        owner = order
        out_shape = jax.ShapeDtypeStruct((len(rows), row_count, columns), jnp.float32)
        out_spec = pl.BlockSpec((len(rows), row_count, tile), lambda n, *_: (0, 0, n))
    else:
        in_specs += [pl.BlockSpec((None, row_count, tile), lambda n, *_: (0, 0, n)), whole_spec(shrink)]
        operands += [total, shrink]
        for block in range(row_count // BLOCK):
            in_specs.append(
                pl.BlockSpec(
                    (1, panels.shape[1], tile), lambda n, order, owner, b=block: (owner[b], 0, n)
                )
            )
            operands.append(panels)
        in_specs.append(pl.BlockSpec(memory_space=pl.ANY))
        operands.append(out)
        aliases = {2 + len(operands) - 1: 0}
        out_shape = jax.ShapeDtypeStruct(out.shape, out.dtype)
        out_spec = pl.BlockSpec((row_count, tile), lambda n, order, owner: (order[slices], n))
    flops = 2 * len(rows) * row_count * slices * width * columns
    moved = 2 * slices * width * columns + 2 * len(rows) * slices * row_count * width
    return pl.pallas_call(
        functools.partial(
            project_kernel,
            {"arrays": len(arrays), "rows": grid_places},
            slices,
            total is not None,
        ),
        grid_spec=pltpu.PrefetchScalarGridSpec(
            num_scalar_prefetch=2,
            grid=(columns // tile,),
            in_specs=in_specs,
            out_specs=out_spec,
        ),
        out_shape=out_shape,
        input_output_aliases=aliases,
        cost_estimate=pl.CostEstimate(
            flops=flops,
            bytes_accessed=moved + 4 * len(rows) * row_count * columns,
            transcendentals=0,
        ),
        compiler_params=pltpu.CompilerParams(vmem_limit_bytes=56 * MIB),
        name=name,
    )(order, owner, *operands)


def shrink_kernel(places, count, owner_ref, *refs):
    arrays, panels_ref, out_ref = refs[:count], refs[count], refs[count + 1]
    rank = panels_ref.shape[1]
    nt = (((1,), (1,)), ((), ()))
    for number, (first, second) in enumerate(places):
        one, two = read(arrays, first), read(arrays, second)
        half = one.shape[1]
        for block in range(one.shape[0] // BLOCK):
            panel = panels_ref[owner_ref[number * (one.shape[0] // BLOCK) + block]]
            span = slice(block * BLOCK, (block + 1) * BLOCK)
            out_ref[number, :, block * rank : (block + 1) * rank] = lax.dot_general(
                one[span], panel[:, :half], nt, preferred_element_type=jnp.float32
            ) + lax.dot_general(
                two[span], panel[:, half:], nt, preferred_element_type=jnp.float32
            )


def shrink_parts(pairs, panels, owner):
    arrays, places = gather_refs([piece for pair in pairs for piece in pair])
    places = [(places[2 * i], places[2 * i + 1]) for i in range(len(pairs))]
    row_count = arrays[0].shape[-2]
    rank = panels.shape[1]
    shape = (len(pairs), BLOCK, rank * (row_count // BLOCK))
    return pl.pallas_call(
        functools.partial(shrink_kernel, places, len(arrays)),
        grid_spec=pltpu.PrefetchScalarGridSpec(
            num_scalar_prefetch=1,
            grid=(1,),
            in_specs=[whole_spec(a) for a in arrays] + [whole_spec(panels)],
            out_specs=pl.BlockSpec(shape, lambda n, *_: (0, 0, 0)),
        ),
        out_shape=jax.ShapeDtypeStruct(shape, jnp.float32),
        cost_estimate=pl.CostEstimate(
            flops=8 * len(pairs) * row_count * panels.shape[2] * rank,
            bytes_accessed=2 * (len(pairs) * row_count * panels.shape[2] + panels.size),
            transcendentals=0,
        ),
        compiler_params=pltpu.CompilerParams(vmem_limit_bytes=56 * MIB),
        name="shrink_parts",
    )(owner, *arrays, panels)


def finish_kernel(order_ref, owner_ref, total_ref, shrink_ref, panel_ref, out_ref):
    rank = panel_ref.shape[1]
    blocks = shrink_ref.shape[2] // rank
    block = pl.program_id(0) % blocks
    shrink = shrink_ref[0, :, :rank]
    for other in range(1, blocks):
        shrink = jnp.where(block == other, shrink_ref[0, :, other * rank : (other + 1) * rank], shrink)
    update = jnp.dot(shrink, panel_ref[0], preferred_element_type=jnp.float32)
    out_ref[...] = (total_ref[0] + adapter_scale * update).astype(out_ref.dtype)


def finish(total, shrink, panels, place, owner, out, row_total):
    sets, row_count, columns = total.shape
    blocks = row_count // BLOCK
    rank = panels.shape[1]
    operands = [total, shrink, panels]
    return pl.pallas_call(
        finish_kernel,
        grid_spec=pltpu.PrefetchScalarGridSpec(
            num_scalar_prefetch=2,
            grid=(sets * blocks,),
            in_specs=[
                pl.BlockSpec((1, BLOCK, columns), lambda i, *_: (i // blocks, i % blocks, 0)),
                pl.BlockSpec((1, BLOCK, rank * blocks), lambda i, *_: (i // blocks, 0, 0)),
                pl.BlockSpec((1, rank, columns), lambda i, place, owner: (owner[i], 0, 0)),
            ],
            out_specs=pl.BlockSpec(
                (BLOCK, columns), lambda i, place, owner: (place[i // blocks] * blocks + i % blocks, 0)
            ),
        ),
        out_shape=jax.ShapeDtypeStruct((row_total, columns), jnp.bfloat16),
        cost_estimate=pl.CostEstimate(
            flops=8 * sets * row_count * rank * columns,
            bytes_accessed=6 * sets * row_count * columns,
            transcendentals=0,
        ),
        name="finish_rows",
    )(place, owner, *operands)


def square(tokens, frozen_weight, down_weight, up_weight, owners, select_slot):
    group = lax.axis_index("grp")
    member = lax.axis_index("tp")
    local_rows, width = tokens.shape
    blocks_own = local_rows // BLOCK
    blocks_here = 4 * blocks_own
    half = width // 8
    send = lambda x, m: lax.ppermute(x, "tp", [(i, i ^ m) for i in range(4)])
    exchange = lambda x: lax.all_to_all(x, "grp", split_axis=0, concat_axis=0, tiled=True)

    def cut(j, second):
        at = ((member ^ 3 ^ j) * 2 + second) * half
        return lax.dynamic_slice(tokens, (0, at), (local_rows, half))

    a = [cut(j, 0) for j in range(4)]
    b = [cut(j, 1) for j in range(4)]
    stack_a, stack_b = jnp.stack([a[0], a[2], a[3]]), jnp.stack([b[0], b[1], b[3]])

    xa, xb, ya, yb, da, db = {}, {}, {}, {}, {}, {}
    xa[0], yb[0] = Piece(send(a[0], 1)), Piece(send(b[0], 2))
    xa[2], yb[1] = Piece(send(a[2], 1)), Piece(send(b[1], 2))
    xb[2], ya[1] = Piece(send(b[2], 1)), Piece(send(a[1], 2))
    db[0], da[0] = Piece(send(yb[0].value(), 1)), Piece(send(xa[0].value(), 2))
    x_rest, y_rest = send(stack_b, 1), send(stack_a, 2)
    for place, j in enumerate((0, 1, 3)):
        xb[j] = Piece(x_rest, place)
    for place, j in enumerate((0, 2, 3)):
        ya[j] = Piece(y_rest, place)
    xa[1], yb[2] = Piece(send(a[1], 1)), Piece(send(b[2], 2))
    xa[3], yb[3] = Piece(send(a[3], 1)), Piece(send(b[3], 2))
    db[1], da[2] = Piece(send(yb[1].value(), 1)), Piece(send(xa[2].value(), 2))
    db[2], da[1] = Piece(send(yb[2].value(), 1)), Piece(send(xa[1].value(), 2))
    db[3], da[3] = Piece(send(yb[3].value(), 1)), Piece(send(xa[3].value(), 2))

    down_tile = exchange(pick(down_weight, select_slot))
    up_tile = exchange(pick(up_weight, select_slot))

    members = member ^ jnp.arange(4, dtype=jnp.int32)
    mine = lax.dynamic_slice_in_dim(owners, group * blocks_here, blocks_here).reshape(4, blocks_own)
    owner = jnp.take(mine, members, axis=0).reshape(-1)

    share = shrink_parts(
        [
            (Piece(a[3]), Piece(b[3])),
            (xa[2], xb[2]),
            (ya[1], yb[1]),
            (da[0], db[0]),
        ],
        down_tile,
        owner,
    )
    home = share[0] + send(share[1], 1) + send(share[2], 2) + send(share[3], 3)
    home = home.astype(jnp.bfloat16)
    shrink = [home] + [send(home, m) for m in (1, 2, 3)]

    slices = jnp.arange(4, dtype=jnp.int32)
    own = project(
        [[(Piece(a[j]), Piece(b[j])) for j in range(4)]],
        member ^ 3 ^ slices,
        frozen_weight,
        tile_of(frozen_weight.shape[1], 256),
        name="own_rows",
    )
    near = project(
        [[(xa[j], xb[j]) for j in range(4)], [(ya[j ^ 3], yb[j ^ 3]) for j in range(4)]],
        member ^ 2 ^ slices,
        frozen_weight,
        tile_of(frozen_weight.shape[1], 256),
        name="near_rows",
    )
    far = project(
        [[(da[j], db[j]) for j in range(3)]],
        member ^ slices,
        frozen_weight,
        tile_of(frozen_weight.shape[1], 256),
        name="far_rows",
    )
    totals = jnp.concatenate([own, near])
    out = finish(
        totals,
        jnp.stack(shrink[:3]),
        up_tile,
        members[:3],
        owner[: 3 * blocks_own],
        None,
        4 * local_rows,
    )
    return project(
        [[(da[3], db[3])]],
        jnp.stack([member ^ 3, member ^ 3]),
        frozen_weight,
        tile_of(frozen_weight.shape[1], 512),
        total=far,
        shrink=shrink[3],
        panels=up_tile,
        owner=owner[3 * blocks_own :],
        out=out,
        name="last_rows",
    )


def general(tokens, frozen_weight, down_weight, up_weight, owners, select_slot):
    tp_count = lax.axis_size("tp")
    group = lax.axis_index("grp")
    member = lax.axis_index("tp")
    local_rows, width = tokens.shape
    group_rows = local_rows * tp_count
    blocks_here = group_rows // BLOCK
    rank_columns = down_weight.shape[1]
    column_slice = up_weight.shape[2]
    my_owners = lax.dynamic_slice_in_dim(owners, group * blocks_here, blocks_here)
    arrived_a, arrived_b = (
        lax.all_to_all(
            jnp.take(panels, select_slot, axis=0), "grp", split_axis=0, concat_axis=0, tiled=True
        )
        for panels in (down_weight, up_weight)
    )
    down_tile = jnp.take(arrived_a, my_owners, axis=0)
    up_tile = jnp.take(arrived_b, my_owners, axis=0)
    whole_a = lax.all_gather(down_tile, "tp", axis=2, tiled=True)
    span_rows = min(local_rows, BLOCK)
    pieces_here = local_rows // span_rows
    first_block = member * local_rows // BLOCK
    local_a = lax.dynamic_slice_in_dim(whole_a, first_block, pieces_here, 0)
    shrink_local = jnp.einsum(
        "pnd,prd->pnr",
        tokens.reshape(pieces_here, span_rows, width),
        local_a,
        preferred_element_type=jnp.float32,
    )
    shrink_local = shrink_local.astype(jnp.bfloat16).reshape(local_rows, rank_columns)
    shrink = lax.all_gather(shrink_local, "tp", axis=0, tiled=True)
    frozen_rows = jnp.dot(
        lax.all_gather(tokens, "tp", axis=0, tiled=True),
        frozen_weight,
        preferred_element_type=jnp.float32,
    )
    update_rows = jnp.einsum(
        "bnr,brc->bnc",
        shrink.reshape(blocks_here, BLOCK, rank_columns),
        up_tile,
        preferred_element_type=jnp.float32,
    )
    update_rows = update_rows.reshape(group_rows, column_slice)
    return (frozen_rows + adapter_scale * update_rows).astype(jnp.bfloat16)


def local(tokens, frozen_weight, down_weight, up_weight, adapter_storage_slot, adapter_of_block):
    group_count = lax.axis_size("grp")
    group = lax.axis_index("grp")
    loaded_here = down_weight.shape[0]
    slot_numbers = jnp.take(adapter_storage_slot, adapter_of_block, axis=0)
    owners = slot_numbers // loaded_here
    offsets = slot_numbers % loaded_here
    owned_here = owners.reshape(group_count, -1) == group
    select_slot = jnp.sum(jnp.where(owned_here, offsets.reshape(group_count, -1), 0), axis=1)
    fits = lax.axis_size("tp") == 4 and tokens.shape[0] % BLOCK == 0
    way = square if fits else general
    return way(tokens, frozen_weight, down_weight, up_weight, owners, select_slot)


def solution(mesh):
    placed = (
        P(("grp", "tp"), None),
        P(None, "tp"),
        P("grp", None, "tp"),
        P("grp", None, "tp"),
        P(),
        P(),
    )
    return jax.shard_map(
        local, mesh=mesh, in_specs=placed, out_specs=P("grp", "tp"), check_vma=False
    )
```

```python
import functools

import jax
import jax.numpy as jnp
from jax import lax
from jax.experimental import pallas as pl
from jax.experimental.pallas import tpu as pltpu
from jax.sharding import PartitionSpec as P

BLOCK = 128
MIB = 1 << 20
PANELS_AT = 4

adapter_scale = 0.5


def tile_of(columns, most):
    return max(t for t in range(128, most + 1, 128) if columns % t == 0)


def whole_spec(array):
    zeros = (0,) * array.ndim
    return pl.BlockSpec(array.shape, lambda *_: zeros)


def cost(flops, moved):
    return pl.CostEstimate(flops=flops, bytes_accessed=moved, transcendentals=0)


class Arrays:
    def __init__(self):
        self.arrays = []

    def place(self, array):
        for number, known in enumerate(self.arrays):
            if known is array:
                return number
        self.arrays.append(array)
        return len(self.arrays) - 1


def view(ref, at):
    if at is None:
        return ref[...]
    return ref[:, at[0] : at[1]] if isinstance(at, tuple) else ref[at]


def cut_kernel(slices_ref, tokens_ref, out_ref):
    out_ref[0] = tokens_ref[...]


def cut_stack(tokens, slices, parts):
    rows, width = tokens.shape
    count, part, band = slices.shape[0], width // parts, rows * parts // 8
    return pl.pallas_call(
        cut_kernel,
        grid_spec=pltpu.PrefetchScalarGridSpec(
            num_scalar_prefetch=1,
            grid=(count, rows // band),
            in_specs=[pl.BlockSpec((band, part), lambda i, r, slices: (r, slices[i]))],
            out_specs=pl.BlockSpec((1, band, part), lambda i, r, slices: (i, r, 0)),
        ),
        out_shape=jax.ShapeDtypeStruct((count, rows, part), tokens.dtype),
        cost_estimate=cost(0, 4 * count * rows * part),
        name="cut_stack",
    )(slices, tokens)


def project_kernel(sets, weights_at, totals_at, update, plan_ref, *refs):
    out_ref = refs[-1]
    for number, terms in enumerate(sets):
        total = None
        for array, at, weight in terms:
            part = jnp.dot(
                view(refs[array], at), refs[weights_at + weight][...], preferred_element_type=jnp.float32
            )
            total = part if total is None else total + part
        if totals_at:
            before = refs[totals_at[number]][...]
            total = before if total is None else total + before
        if update is None:
            out_ref[number] = total
        else:
            first_set, shrinks_at, panels_at = update
            shrink = 0
            for at in shrinks_at:
                shrink += refs[at][plan_ref[first_set + number]].astype(jnp.float32)
            shrink = shrink.astype(jnp.bfloat16)
            for block, panel in enumerate(panels_at):
                rank = refs[panel].shape[0]
                term = jnp.dot(
                    shrink[:, block * rank : (block + 1) * rank],
                    refs[panel][...],
                    preferred_element_type=jnp.float32,
                )
                span = slice(block * BLOCK, (block + 1) * BLOCK)
                out_ref[span, :] = (total[span] + adapter_scale * term).astype(out_ref.dtype)


def project(sets, weight, tile, plan, rows, total=None, update=None, into=None, weigh=2, name=None):
    columns = weight.shape[1]
    known, halves, flat = Arrays(), [], []
    for terms in sets:
        flat.append([])
        for array, at, k, half in terms:
            if (k, half) not in halves:
                halves.append((k, half))
            flat[-1].append((known.place(array), at, halves.index((k, half))))
    depth = weight.shape[0] // 4
    operands = list(known.arrays)
    in_specs = [whole_spec(a) for a in operands]
    weights_at = len(operands)
    for k, half in halves:
        if k is None:
            in_specs.append(pl.BlockSpec((depth, tile), lambda n, plan, half=half: (half, n)))
        elif half is None:
            in_specs.append(pl.BlockSpec((depth, tile), lambda n, plan, k=k: (plan[k], n)))
        else:
            in_specs.append(
                pl.BlockSpec((depth // 2, tile), lambda n, plan, k=k, half=half: (plan[k] * 2 + half, n))
            )
        operands.append(weight)
    totals_at = []
    if total is not None:
        for number in range(len(sets)):
            in_specs.append(pl.BlockSpec((None, rows, tile), lambda n, plan, number=number: (number, 0, n)))
            operands.append(total)
            totals_at.append(len(operands) - 1)
    updating, aliases = None, {}
    if update is None:
        out_shape = jax.ShapeDtypeStruct((len(sets), rows, columns), jnp.float32)
        out_spec = pl.BlockSpec((len(sets), rows, tile), lambda n, plan: (0, 0, n))
    else:
        first_set, shrinks, panels = update
        shrinks_at, panels_at = [], []
        for shrink in shrinks:
            in_specs.append(whole_spec(shrink))
            operands.append(shrink)
            shrinks_at.append(len(operands) - 1)
        for block in range(rows // BLOCK):
            index = PANELS_AT + first_set * (rows // BLOCK) + block
            in_specs.append(
                pl.BlockSpec((None, panels.shape[1], tile), lambda n, plan, index=index: (plan[index], 0, n))
            )
            operands.append(panels)
            panels_at.append(len(operands) - 1)
        updating = (first_set, shrinks_at, panels_at)
        out_shape = jax.ShapeDtypeStruct(into.shape, into.dtype)
        out_spec = pl.BlockSpec((rows, tile), lambda n, plan: (plan[first_set], n))
        in_specs.append(pl.BlockSpec(memory_space=pl.ANY))
        operands.append(into)
        aliases = {len(operands): 0}
    products = sum(2 if half is None or k is None else 1 for terms in sets for _, _, k, half in terms)
    products *= rows * depth // 2
    moved = 2 * products // rows * columns + 4 * len(sets) * rows * columns * (1 if total is None else 2)
    return pl.pallas_call(
        functools.partial(project_kernel, flat, weights_at, totals_at, updating),
        grid_spec=pltpu.PrefetchScalarGridSpec(
            num_scalar_prefetch=1,
            grid=(columns // tile,),
            in_specs=in_specs,
            out_specs=out_spec,
        ),
        out_shape=out_shape,
        input_output_aliases=aliases,
        cost_estimate=cost(weigh * 2 * products * columns, weigh * moved),
        compiler_params=pltpu.CompilerParams(vmem_limit_bytes=56 * MIB),
        name=name,
    )(plan, *operands)


def finish_kernel(count, plan_ref, *refs):
    own_ref, near_ref, panel_one, panel_two, out_ref = refs[0], refs[1], refs[-3], refs[-2], refs[-1]
    number = pl.program_id(0)
    shrink = 0
    for ref in refs[2:-3]:
        shrink += ref[plan_ref[number]].astype(jnp.float32)
    shrink = shrink.astype(jnp.bfloat16)
    rank = panel_one.shape[0]
    for block, panel in enumerate((panel_one, panel_two)):
        term = adapter_scale * jnp.dot(
            shrink[:, block * rank : (block + 1) * rank], panel[...], preferred_element_type=jnp.float32
        )
        span = slice(block * BLOCK, (block + 1) * BLOCK)

        @pl.when(number == 0)
        def _():
            out_ref[span, :] = (own_ref[span] + term).astype(out_ref.dtype)

        @pl.when(number != 0)
        def _():
            out_ref[span, :] = (near_ref[span] + term).astype(out_ref.dtype)


def finish(own, near, shrinks, panels, plan, row_total):
    _, rows, columns = near.shape
    rank = panels.shape[1]
    tile = tile_of(columns, 2560)
    return pl.pallas_call(
        functools.partial(finish_kernel, 3),
        grid_spec=pltpu.PrefetchScalarGridSpec(
            num_scalar_prefetch=1,
            grid=(3, columns // tile),
            in_specs=[
                pl.BlockSpec((None, rows, tile), lambda s, n, plan: (0, 0, jnp.where(s == 0, n, columns // tile - 1))),
                pl.BlockSpec((None, rows, tile), lambda s, n, plan: (jnp.maximum(s - 1, 0), 0, n)),
            ]
            + [whole_spec(shrink) for shrink in shrinks]
            + [
                pl.BlockSpec(
                    (None, rank, tile), lambda s, n, plan, block=block: (plan[PANELS_AT + 2 * s + block], 0, n)
                )
                for block in range(2)
            ],
            out_specs=pl.BlockSpec((rows, tile), lambda s, n, plan: (plan[s], n)),
        ),
        out_shape=jax.ShapeDtypeStruct((row_total, columns), jnp.bfloat16),
        cost_estimate=cost(12 * rows * rank * columns, 18 * rows * columns),
        compiler_params=pltpu.CompilerParams(vmem_limit_bytes=56 * MIB),
        name="finish_rows",
    )(plan, own, near, *shrinks, panels, panels)


def shrink_kernel(sets, panels_at, plan_ref, *refs):
    panels_ref, out_ref = refs[panels_at], refs[-1]
    rank = panels_ref.shape[1]
    nt = (((1,), (1,)), ((), ()))
    for number, terms in enumerate(sets):
        blocks = refs[terms[0][0]].shape[-2] // BLOCK
        for block in range(blocks):
            panel = plan_ref[PANELS_AT + number * blocks + block]
            total = 0
            for array, at, start in terms:
                tokens = view(refs[array], at)[block * BLOCK : (block + 1) * BLOCK]
                total += lax.dot_general(
                    tokens,
                    panels_ref[panel, :, start : start + tokens.shape[1]],
                    nt,
                    preferred_element_type=jnp.float32,
                )
            out_ref[plan_ref[number], :, block * rank : (block + 1) * rank] = total.astype(
                out_ref.dtype
            )


def shrink_parts(tokens, sets, panels, plan):
    rows, width = tokens.shape
    known = Arrays()
    flat = [[(known.place(tokens), None, 0)]]
    flat += [[(known.place(array), at, start) for array, at, start in terms] for terms in sets]
    operands = known.arrays + [panels]
    _, rank, depth = panels.shape
    shape = (len(flat), BLOCK, rank * (rows // BLOCK))
    in_specs = [whole_spec(a) for a in operands]
    in_specs[0] = pl.BlockSpec((rows, depth), lambda i, plan: (0, plan[0]))
    return pl.pallas_call(
        functools.partial(shrink_kernel, flat, len(known.arrays)),
        grid_spec=pltpu.PrefetchScalarGridSpec(
            num_scalar_prefetch=1,
            grid=(1,),
            in_specs=in_specs,
            out_specs=pl.BlockSpec(shape, lambda *_: (0, 0, 0)),
        ),
        out_shape=jax.ShapeDtypeStruct(shape, tokens.dtype),
        cost_estimate=cost(8 * len(flat) * rows * depth * rank, 2 * (panels.size + len(flat) * rows * depth)),
        compiler_params=pltpu.CompilerParams(vmem_limit_bytes=56 * MIB),
        name="shrink_parts",
    )(plan, *operands)


def after(value, *others):
    return lax.optimization_barrier((value,) + others)[0]


def square(tokens, frozen_weight, down_weight, up_weight, owners, select_slot):
    group = lax.axis_index("grp")
    member = lax.axis_index("tp")
    rows, width = tokens.shape
    blocks = rows // BLOCK
    depth, half = width // 4, width // 8
    to_x = lambda v: lax.ppermute(v, "tp", [(i, i ^ 1) for i in range(4)])
    to_y = lambda v: lax.ppermute(v, "tp", [(i, i ^ 2) for i in range(4)])
    across = lambda v: lax.ppermute(v, "tp", [(i, i ^ 3) for i in range(4)])
    first, second = (0, half), (half, depth)

    members = member ^ jnp.arange(4, dtype=jnp.int32)
    mine = lax.dynamic_slice_in_dim(owners, group * 4 * blocks, 4 * blocks).reshape(4, blocks)
    mine = jnp.sum(jnp.where((members[:, None] == jnp.arange(4))[:, :, None], mine[None], 0), axis=1)
    plan = jnp.concatenate([members, mine.reshape(-1)]).astype(jnp.int32)

    def cut(j, second):
        return lax.dynamic_slice(tokens, (0, (member ^ 3 ^ j) * depth + second * half), (rows, half))

    def eighths(*places):
        numbers = jnp.stack([(member ^ 3 ^ j) * 2 + second for j, second in places])
        return cut_stack(tokens, numbers.astype(jnp.int32), 8)

    a0, b0 = cut(0, 0), cut(0, 1)
    xa0, yb0 = to_x(a0), to_y(b0)
    early_x, early_y = eighths((0, 1), (3, 0), (3, 1)), eighths((0, 0), (3, 0), (3, 1))
    x_early, y_early = to_x(early_x), to_y(early_y)
    late = cut_stack(tokens, jnp.stack([member ^ 2, member ^ 1]).astype(jnp.int32), 4)
    x12, y12 = to_x(late), to_y(late)

    def chosen(panels, select):
        return jnp.take(panels, select, axis=0, mode="clip")

    def exchange(panels):
        return lax.all_to_all(panels, "grp", split_axis=0, concat_axis=0, tiled=True)

    down_out = chosen(down_weight, after(select_slot, xa0, yb0, early_x, early_y))
    down = exchange(down_out)

    own = project(
        [[(tokens, (i * depth, (i + 1) * depth), None, i) for i in range(4)]],
        frozen_weight, tile_of(frozen_weight.shape[1], 512), after(plan, down_out, late), rows, weigh=0, name="own_rows",
    )

    tile = tile_of(frozen_weight.shape[1], 512)
    near = project(
        [
            [(xa0, None, 2, 0), (x_early, 0, 2, 1), (x_early, 1, 1, 0), (x_early, 2, 1, 1)],
            [(y_early, 1, 2, 0), (y_early, 2, 2, 1), (y_early, 0, 1, 0), (yb0, None, 1, 1)],
        ],
        frozen_weight, tile, after(plan, own), rows, weigh=0, name="near_rows",
    )
    up = exchange(chosen(up_weight, after(select_slot, down, near)))

    da0, db0 = to_y(after(xa0, x_early, y_early)), to_x(after(yb0, x_early, y_early))
    da3, db3 = to_y(after(x_early[1], near)), to_x(after(y_early[2], near))
    near = project(
        [[(x12, 0, 3, None), (x12, 1, 0, None)], [(y12, 1, 3, None), (y12, 0, 0, None)]],
        frozen_weight, tile, plan, rows, total=near, name="near_rows_rest",
    )

    share = shrink_parts(
        tokens,
        [[(x12, 1, 0)], [(y12, 0, 0)], [(da0, None, 0), (db0, None, half)]],
        down,
        after(plan, near),
    )
    shrinks = [share, to_x(share), to_y(share), across(share)]
    da12 = to_y(after(x12[:, :, :half], share))
    db12 = to_x(after(y12[:, :, half:], share))

    far = project(
        [[(da0, None, 0, 0), (db0, None, 0, 1), (da3, None, 3, 0), (db3, None, 3, 1)]],
        frozen_weight, tile_of(frozen_weight.shape[1], 640), after(plan, share), rows, name="far_rows",
    )
    out = finish(own, near, shrinks, up, after(plan, far), 4 * rows)
    return project(
        [[(da12, 0, 1, 0), (db12, 0, 1, 1), (da12, 1, 2, 0), (db12, 1, 2, 1)]],
        frozen_weight, tile_of(frozen_weight.shape[1], 640), plan, rows,
        total=far, update=(3, shrinks, up), into=out, name="last_rows",
    )


def general(tokens, frozen_weight, down_weight, up_weight, owners, select_slot):
    tp_count = lax.axis_size("tp")
    group = lax.axis_index("grp")
    member = lax.axis_index("tp")
    local_rows, width = tokens.shape
    group_rows = local_rows * tp_count
    blocks_here = group_rows // BLOCK
    rank_columns = down_weight.shape[1]
    column_slice = up_weight.shape[2]
    my_owners = lax.dynamic_slice_in_dim(owners, group * blocks_here, blocks_here)
    arrived_a, arrived_b = (
        lax.all_to_all(
            jnp.take(panels, select_slot, axis=0), "grp", split_axis=0, concat_axis=0, tiled=True
        )
        for panels in (down_weight, up_weight)
    )
    down_tile = jnp.take(arrived_a, my_owners, axis=0)
    up_tile = jnp.take(arrived_b, my_owners, axis=0)
    whole_a = lax.all_gather(down_tile, "tp", axis=2, tiled=True)
    span_rows = min(local_rows, BLOCK)
    pieces_here = local_rows // span_rows
    first_block = member * local_rows // BLOCK
    local_a = lax.dynamic_slice_in_dim(whole_a, first_block, pieces_here, 0)
    shrink_local = jnp.einsum(
        "pnd,prd->pnr",
        tokens.reshape(pieces_here, span_rows, width),
        local_a,
        preferred_element_type=jnp.float32,
    )
    shrink_local = shrink_local.astype(jnp.bfloat16).reshape(local_rows, rank_columns)
    shrink = lax.all_gather(shrink_local, "tp", axis=0, tiled=True)
    frozen_rows = jnp.dot(
        lax.all_gather(tokens, "tp", axis=0, tiled=True),
        frozen_weight,
        preferred_element_type=jnp.float32,
    )
    update_rows = jnp.einsum(
        "bnr,brc->bnc",
        shrink.reshape(blocks_here, BLOCK, rank_columns),
        up_tile,
        preferred_element_type=jnp.float32,
    )
    update_rows = update_rows.reshape(group_rows, column_slice)
    return (frozen_rows + adapter_scale * update_rows).astype(jnp.bfloat16)


def local(tokens, frozen_weight, down_weight, up_weight, adapter_storage_slot, adapter_of_block):
    group_count = lax.axis_size("grp")
    group = lax.axis_index("grp")
    loaded_here = down_weight.shape[0]
    adapters = jnp.arange(adapter_storage_slot.shape[0])
    named = adapter_of_block[:, None] == adapters[None, :]
    slot_numbers = jnp.sum(jnp.where(named, adapter_storage_slot[None, :], 0), axis=1)
    owners = slot_numbers // loaded_here
    offsets = slot_numbers % loaded_here
    owned_here = owners.reshape(group_count, -1) == group
    select_slot = jnp.sum(jnp.where(owned_here, offsets.reshape(group_count, -1), 0), axis=1)
    fits = lax.axis_size("tp") == 4 and tokens.shape[0] % BLOCK == 0
    way = square if fits else general
    return way(tokens, frozen_weight, down_weight, up_weight, owners, select_slot)


def solution(mesh):
    placed = (
        P(("grp", "tp"), None),
        P(None, "tp"),
        P("grp", None, "tp"),
        P("grp", None, "tp"),
        P(),
        P(),
    )
    return jax.shard_map(
        local, mesh=mesh, in_specs=placed, out_specs=P("grp", "tp"), check_vma=False
    )
```

```python
import functools

import jax
import jax.numpy as jnp
from jax import lax
from jax.experimental import pallas as pl
from jax.experimental.pallas import tpu as pltpu
from jax.sharding import PartitionSpec as P

BLOCK = 128
MIB = 1 << 20
PANELS_AT = 4

adapter_scale = 0.5


def tile_of(columns, most):
    return max(t for t in range(128, most + 1, 128) if columns % t == 0)


def whole_spec(array):
    zeros = (0,) * array.ndim
    return pl.BlockSpec(array.shape, lambda *_: zeros)


def cost(flops, moved):
    return pl.CostEstimate(flops=flops, bytes_accessed=moved, transcendentals=0)


class Arrays:
    def __init__(self):
        self.arrays = []

    def place(self, array):
        for number, known in enumerate(self.arrays):
            if known is array:
                return number
        self.arrays.append(array)
        return len(self.arrays) - 1


def view(ref, at):
    if at is None:
        return ref[...]
    return ref[:, at[0] : at[1]] if isinstance(at, tuple) else ref[at]


def cut_kernel(columns_ref, *refs):
    stacks = len(refs) // 2
    for source, out in zip(refs[:stacks], refs[stacks:]):
        out[0] = source[...]


def cut_stacks(tokens, columns, stacks):
    rows, width = tokens.shape
    count, part = columns.shape[0] // stacks, width // 8
    return pl.pallas_call(
        cut_kernel,
        grid_spec=pltpu.PrefetchScalarGridSpec(
            num_scalar_prefetch=1,
            grid=(count,),
            in_specs=[
                pl.BlockSpec((rows, part), lambda i, columns, first=stack * count: (0, columns[first + i]))
                for stack in range(stacks)
            ],
            out_specs=[pl.BlockSpec((1, rows, part), lambda i, columns: (i, 0, 0))] * stacks,
        ),
        out_shape=[jax.ShapeDtypeStruct((count, rows, part), tokens.dtype)] * stacks,
        cost_estimate=cost(0, 4 * stacks * count * rows * part),
        name="cut_stacks",
    )(columns, *[tokens] * stacks)


def project_kernel(sets, weights_at, totals_at, update, plan_ref, *refs):
    out_ref = refs[-1]
    for number, terms in enumerate(sets):
        total = None
        for array, at, weight in terms:
            part = jnp.dot(
                view(refs[array], at), refs[weights_at + weight][...], preferred_element_type=jnp.float32
            )
            total = part if total is None else total + part
        if totals_at:
            before = refs[totals_at[number]][...]
            total = before if total is None else total + before
        if update is None:
            out_ref[number] = total
        else:
            shrink_at, panels_at = update
            shrink = refs[shrink_at][...]
            for block, panel in enumerate(panels_at):
                rank = refs[panel].shape[0]
                term = jnp.dot(
                    shrink[:, block * rank : (block + 1) * rank],
                    refs[panel][...],
                    preferred_element_type=jnp.float32,
                )
                span = slice(block * BLOCK, (block + 1) * BLOCK)
                out_ref[span, :] = (total[span] + adapter_scale * term).astype(out_ref.dtype)


def project(sets, weight, tile, plan, rows, total=None, update=None, into=None, weigh=2, name=None):
    columns = weight.shape[1]
    known, halves, flat = Arrays(), [], []
    for terms in sets:
        flat.append([])
        for array, at, k, half in terms:
            if (k, half) not in halves:
                halves.append((k, half))
            flat[-1].append((known.place(array), at, halves.index((k, half))))
    depth = weight.shape[0] // 4
    operands = list(known.arrays)
    in_specs = [whole_spec(a) for a in operands]
    weights_at = len(operands)
    for k, half in halves:
        if k is None:
            in_specs.append(pl.BlockSpec((depth, tile), lambda n, plan, half=half: (half, n)))
        elif half is None:
            in_specs.append(pl.BlockSpec((depth, tile), lambda n, plan, k=k: (plan[k], n)))
        else:
            in_specs.append(
                pl.BlockSpec((depth // 2, tile), lambda n, plan, k=k, half=half: (plan[k] * 2 + half, n))
            )
        operands.append(weight)
    totals_at = []
    if total is not None:
        for number in range(len(sets)):
            in_specs.append(pl.BlockSpec((None, rows, tile), lambda n, plan, number=number: (number, 0, n)))
            operands.append(total)
            totals_at.append(len(operands) - 1)
    updating, aliases = None, {}
    if update is None:
        out_shape = jax.ShapeDtypeStruct((len(sets), rows, columns), jnp.float32)
        out_spec = pl.BlockSpec((len(sets), rows, tile), lambda n, plan: (0, 0, n))
    else:
        first_set, shrink, panels = update
        in_specs.append(whole_spec(shrink))
        operands.append(shrink)
        shrink_at, panels_at = len(operands) - 1, []
        for block in range(rows // BLOCK):
            index = PANELS_AT + first_set * (rows // BLOCK) + block
            in_specs.append(
                pl.BlockSpec((None, panels.shape[1], tile), lambda n, plan, index=index: (plan[index], 0, n))
            )
            operands.append(panels)
            panels_at.append(len(operands) - 1)
        updating = (shrink_at, panels_at)
        out_shape = jax.ShapeDtypeStruct(into.shape, into.dtype)
        out_spec = pl.BlockSpec((rows, tile), lambda n, plan: (plan[first_set], n))
        in_specs.append(pl.BlockSpec(memory_space=pl.ANY))
        operands.append(into)
        aliases = {len(operands): 0}
    products = sum(2 if half is None or k is None else 1 for terms in sets for _, _, k, half in terms)
    products *= rows * depth // 2
    moved = 2 * products // rows * columns + 4 * len(sets) * rows * columns * (1 if total is None else 2)
    return pl.pallas_call(
        functools.partial(project_kernel, flat, weights_at, totals_at, updating),
        grid_spec=pltpu.PrefetchScalarGridSpec(
            num_scalar_prefetch=1,
            grid=(columns // tile,),
            in_specs=in_specs,
            out_specs=out_spec,
        ),
        out_shape=out_shape,
        input_output_aliases=aliases,
        cost_estimate=cost(weigh * 2 * products * columns, weigh * moved),
        compiler_params=pltpu.CompilerParams(vmem_limit_bytes=32 * MIB),
        name=name,
    )(plan, *operands)


def finish_kernel(count, plan_ref, *refs):
    own_ref, near_ref, panel_one, panel_two, out_ref = refs[0], refs[1], refs[-3], refs[-2], refs[-1]
    number = pl.program_id(0)
    shrink = refs[2][...]
    for other in range(1, count):
        shrink = jnp.where(number == other, refs[2 + other][...], shrink)
    rank = panel_one.shape[0]
    for block, panel in enumerate((panel_one, panel_two)):
        term = adapter_scale * jnp.dot(
            shrink[:, block * rank : (block + 1) * rank], panel[...], preferred_element_type=jnp.float32
        )
        span = slice(block * BLOCK, (block + 1) * BLOCK)

        @pl.when(number == 0)
        def _():
            out_ref[span, :] = (own_ref[span] + term).astype(out_ref.dtype)

        @pl.when(number != 0)
        def _():
            out_ref[span, :] = (near_ref[span] + term).astype(out_ref.dtype)


def finish(own, near, shrinks, panels, plan, row_total):
    _, rows, columns = near.shape
    rank = panels.shape[1]
    tile = tile_of(columns, 2560)
    return pl.pallas_call(
        functools.partial(finish_kernel, 3),
        grid_spec=pltpu.PrefetchScalarGridSpec(
            num_scalar_prefetch=1,
            grid=(3, columns // tile),
            in_specs=[
                pl.BlockSpec((None, rows, tile), lambda s, n, plan: (0, 0, jnp.where(s == 0, n, columns // tile - 1))),
                pl.BlockSpec((None, rows, tile), lambda s, n, plan: (jnp.maximum(s - 1, 0), 0, n)),
            ]
            + [whole_spec(shrink) for shrink in shrinks]
            + [
                pl.BlockSpec(
                    (None, rank, tile), lambda s, n, plan, block=block: (plan[PANELS_AT + 2 * s + block], 0, n)
                )
                for block in range(2)
            ],
            out_specs=pl.BlockSpec((rows, tile), lambda s, n, plan: (plan[s], n)),
        ),
        out_shape=jax.ShapeDtypeStruct((row_total, columns), jnp.bfloat16),
        cost_estimate=cost(12 * rows * rank * columns, 18 * rows * columns),
        compiler_params=pltpu.CompilerParams(vmem_limit_bytes=32 * MIB),
        name="finish_rows",
    )(plan, own, near, *shrinks, panels, panels)


def shrink_kernel(sets, panels_at, plan_ref, *refs):
    panels_ref = refs[panels_at]
    rank = panels_ref.shape[1]
    nt = (((1,), (1,)), ((), ()))
    for number, (terms, out_ref) in enumerate(zip(sets, refs[panels_at + 1 :])):
        blocks = refs[terms[0][0]].shape[-2] // BLOCK
        for block in range(blocks):
            panel = plan_ref[PANELS_AT + number * blocks + block]
            total = 0
            for array, at, start in terms:
                tokens = view(refs[array], at)[block * BLOCK : (block + 1) * BLOCK]
                total += lax.dot_general(
                    tokens,
                    panels_ref[panel, :, start : start + tokens.shape[1]],
                    nt,
                    preferred_element_type=jnp.float32,
                )
            out_ref[:, block * rank : (block + 1) * rank] = total


def shrink_parts(tokens, sets, panels, plan):
    rows, width = tokens.shape
    known = Arrays()
    flat = [[(known.place(tokens), None, 0)]]
    flat += [[(known.place(array), at, start) for array, at, start in terms] for terms in sets]
    operands = known.arrays + [panels]
    _, rank, depth = panels.shape
    shape = (BLOCK, rank * (rows // BLOCK))
    in_specs = [whole_spec(a) for a in operands]
    in_specs[0] = pl.BlockSpec((rows, depth), lambda i, plan: (0, plan[0]))
    return pl.pallas_call(
        functools.partial(shrink_kernel, flat, len(known.arrays)),
        grid_spec=pltpu.PrefetchScalarGridSpec(
            num_scalar_prefetch=1,
            grid=(1,),
            in_specs=in_specs,
            out_specs=[pl.BlockSpec(shape, lambda *_: (0, 0))] * len(flat),
        ),
        out_shape=[jax.ShapeDtypeStruct(shape, jnp.float32)] * len(flat),
        cost_estimate=cost(8 * len(flat) * rows * depth * rank, 2 * (panels.size + len(flat) * rows * depth)),
        compiler_params=pltpu.CompilerParams(vmem_limit_bytes=32 * MIB),
        name="shrink_parts",
    )(plan, *operands)


def after(value, *others):
    return lax.optimization_barrier((value,) + others)[0]


def square(tokens, frozen_weight, down_weight, up_weight, owners, select_slot):
    group = lax.axis_index("grp")
    member = lax.axis_index("tp")
    rows, width = tokens.shape
    blocks = rows // BLOCK
    depth, half = width // 4, width // 8
    to_x = lambda v: lax.ppermute(v, "tp", [(i, i ^ 1) for i in range(4)])
    to_y = lambda v: lax.ppermute(v, "tp", [(i, i ^ 2) for i in range(4)])
    across = lambda v: lax.ppermute(v, "tp", [(i, i ^ 3) for i in range(4)])
    first, second = (0, half), (half, depth)

    members = member ^ jnp.arange(4, dtype=jnp.int32)
    mine = lax.dynamic_slice_in_dim(owners, group * 4 * blocks, 4 * blocks).reshape(4, blocks)
    mine = jnp.sum(jnp.where((members[:, None] == jnp.arange(4))[:, :, None], mine[None], 0), axis=1)
    plan = jnp.concatenate([members, mine.reshape(-1)]).astype(jnp.int32)

    def eighths(*places):
        return jnp.stack([(member ^ 3 ^ j) * 2 + second for j, second in places]).astype(jnp.int32)

    (s03,) = cut_stacks(tokens, eighths((0, 0), (0, 1), (3, 0), (3, 1)), 1)
    x03, y03 = to_x(s03), to_y(s03)
    a12, b12 = cut_stacks(tokens, eighths((1, 0), (2, 0), (1, 1), (2, 1)), 2)
    xa12, ya12 = to_x(a12), to_y(a12)
    xb12, yb12 = to_x(b12), to_y(b12)

    def chosen(panels, select):
        return jnp.take(panels, select, axis=0, mode="clip")

    def exchange(panels):
        return lax.all_to_all(panels, "grp", split_axis=0, concat_axis=0, tiled=True)

    down_out = chosen(down_weight, after(select_slot, a12, b12))
    down = exchange(down_out)

    own = project(
        [[(tokens, (i * depth, (i + 1) * depth), None, i) for i in range(4)]],
        frozen_weight, tile_of(frozen_weight.shape[1], 512), after(plan, down_out), rows, weigh=0, name="own_rows",
    )

    tile = tile_of(frozen_weight.shape[1], 512)
    near = project(
        [
            [(x03, 0, 2, 0), (x03, 1, 2, 1), (x03, 2, 1, 0), (x03, 3, 1, 1)],
            [(y03, 2, 2, 0), (y03, 3, 2, 1), (y03, 0, 1, 0), (y03, 1, 1, 1)],
        ],
        frozen_weight, tile, after(plan, own), rows, weigh=6, name="near_rows",
    )
    up = exchange(chosen(up_weight, after(select_slot, down, near)))
    near = project(
        [
            [(xa12, 0, 3, 0), (xa12, 1, 0, 0)],
            [(ya12, 1, 3, 0), (ya12, 0, 0, 0)],
        ],
        frozen_weight, tile, plan, rows, total=near, weigh=2, name="near_rows_more",
    )

    da0, db0 = to_y(after(x03[0], xa12, ya12)), to_x(after(y03[1], xa12, ya12))
    da3, db3 = to_y(after(x03[2], near)), to_x(after(y03[3], near))
    near = project(
        [
            [(xb12, 0, 3, 1), (xb12, 1, 0, 1)],
            [(yb12, 1, 3, 1), (yb12, 0, 0, 1)],
        ],
        frozen_weight, tile, plan, rows, total=near, name="near_rows_rest",
    )

    share = shrink_parts(
        tokens,
        [
            [(xa12, 1, 0), (xb12, 1, half)],
            [(ya12, 0, 0), (yb12, 0, half)],
            [(da0, None, 0), (db0, None, half)],
        ],
        down,
        after(plan, near),
    )
    home = share[0] + to_x(share[1]) + to_y(share[2]) + across(share[3])
    home = home.astype(jnp.bfloat16)
    shrinks = [home, to_x(home), to_y(home), across(home)]
    da12, db12 = to_y(after(xa12, home)), to_x(after(yb12, home))

    far = project(
        [[(da0, None, 0, 0), (db0, None, 0, 1), (da3, None, 3, 0), (db3, None, 3, 1)]],
        frozen_weight, tile_of(frozen_weight.shape[1], 640), after(plan, home), rows, name="far_rows",
    )
    out = finish(own, near, shrinks[:3], up, after(plan, far), 4 * rows)
    return project(
        [[(da12, 0, 1, 0), (db12, 0, 1, 1), (da12, 1, 2, 0), (db12, 1, 2, 1)]],
        frozen_weight, tile_of(frozen_weight.shape[1], 640), plan, rows,
        total=far, update=(3, shrinks[3], up), into=out, name="last_rows",
    )


def general(tokens, frozen_weight, down_weight, up_weight, owners, select_slot):
    tp_count = lax.axis_size("tp")
    group = lax.axis_index("grp")
    member = lax.axis_index("tp")
    local_rows, width = tokens.shape
    group_rows = local_rows * tp_count
    blocks_here = group_rows // BLOCK
    rank_columns = down_weight.shape[1]
    column_slice = up_weight.shape[2]
    my_owners = lax.dynamic_slice_in_dim(owners, group * blocks_here, blocks_here)
    arrived_a, arrived_b = (
        lax.all_to_all(
            jnp.take(panels, select_slot, axis=0), "grp", split_axis=0, concat_axis=0, tiled=True
        )
        for panels in (down_weight, up_weight)
    )
    down_tile = jnp.take(arrived_a, my_owners, axis=0)
    up_tile = jnp.take(arrived_b, my_owners, axis=0)
    whole_a = lax.all_gather(down_tile, "tp", axis=2, tiled=True)
    span_rows = min(local_rows, BLOCK)
    pieces_here = local_rows // span_rows
    first_block = member * local_rows // BLOCK
    local_a = lax.dynamic_slice_in_dim(whole_a, first_block, pieces_here, 0)
    shrink_local = jnp.einsum(
        "pnd,prd->pnr",
        tokens.reshape(pieces_here, span_rows, width),
        local_a,
        preferred_element_type=jnp.float32,
    )
    shrink_local = shrink_local.astype(jnp.bfloat16).reshape(local_rows, rank_columns)
    shrink = lax.all_gather(shrink_local, "tp", axis=0, tiled=True)
    frozen_rows = jnp.dot(
        lax.all_gather(tokens, "tp", axis=0, tiled=True),
        frozen_weight,
        preferred_element_type=jnp.float32,
    )
    update_rows = jnp.einsum(
        "bnr,brc->bnc",
        shrink.reshape(blocks_here, BLOCK, rank_columns),
        up_tile,
        preferred_element_type=jnp.float32,
    )
    update_rows = update_rows.reshape(group_rows, column_slice)
    return (frozen_rows + adapter_scale * update_rows).astype(jnp.bfloat16)


def local(tokens, frozen_weight, down_weight, up_weight, adapter_storage_slot, adapter_of_block):
    group_count = lax.axis_size("grp")
    group = lax.axis_index("grp")
    loaded_here = down_weight.shape[0]
    adapters = jnp.arange(adapter_storage_slot.shape[0])
    named = adapter_of_block[:, None] == adapters[None, :]
    slot_numbers = jnp.sum(jnp.where(named, adapter_storage_slot[None, :], 0), axis=1)
    owners = slot_numbers // loaded_here
    offsets = slot_numbers % loaded_here
    owned_here = owners.reshape(group_count, -1) == group
    select_slot = jnp.sum(jnp.where(owned_here, offsets.reshape(group_count, -1), 0), axis=1)
    fits = lax.axis_size("tp") == 4 and tokens.shape[0] % BLOCK == 0
    way = square if fits else general
    return way(tokens, frozen_weight, down_weight, up_weight, owners, select_slot)


def solution(mesh):
    placed = (
        P(("grp", "tp"), None),
        P(None, "tp"),
        P("grp", None, "tp"),
        P("grp", None, "tp"),
        P(),
        P(),
    )
    return jax.shard_map(
        local, mesh=mesh, in_specs=placed, out_specs=P("grp", "tp"), check_vma=False
    )
```

```python
import functools

import jax
import jax.numpy as jnp
from jax import lax
from jax.experimental import pallas as pl
from jax.experimental.pallas import tpu as pltpu
from jax.sharding import PartitionSpec as P

BLOCK = 128
MIB = 1 << 20
PANELS_AT = 4
VMEM_BYTES = 32 * MIB

adapter_scale = 0.5


def tile_of(columns, most):
    return max(t for t in range(128, most + 1, 128) if columns % t == 0)


def whole_spec(array):
    zeros = (0,) * array.ndim
    return pl.BlockSpec(array.shape, lambda *_: zeros)


def cost(flops, moved):
    return pl.CostEstimate(flops=flops, bytes_accessed=moved, transcendentals=0)


class Arrays:
    def __init__(self):
        self.arrays = []

    def place(self, array):
        for number, known in enumerate(self.arrays):
            if known is array:
                return number
        self.arrays.append(array)
        return len(self.arrays) - 1


def view(ref, at):
    if at is None:
        return ref[...]
    return ref[:, at[0] : at[1]] if isinstance(at, tuple) else ref[at]


def project_kernel(sets, weights_at, totals_at, update, plan_ref, *refs):
    out_ref = refs[-1]
    for number, terms in enumerate(sets):
        total = None
        for array, at, weight in terms:
            part = jnp.dot(
                view(refs[array], at), refs[weights_at + weight][...], preferred_element_type=jnp.float32
            )
            total = part if total is None else total + part
        if totals_at:
            before = refs[totals_at[number]][...]
            total = before if total is None else total + before
        if update is None:
            out_ref[number] = total
        else:
            shrink_at, panels_at = update
            shrink = refs[shrink_at][...]
            for block, panel in enumerate(panels_at):
                rank = refs[panel].shape[0]
                term = jnp.dot(
                    shrink[:, block * rank : (block + 1) * rank],
                    refs[panel][...],
                    preferred_element_type=jnp.float32,
                )
                span = slice(block * BLOCK, (block + 1) * BLOCK)
                out_ref[span, :] = (total[span] + adapter_scale * term).astype(out_ref.dtype)


def project(sets, weight, tile, plan, rows, total=None, update=None, into=None, weigh=2, name=None):
    columns = weight.shape[1]
    known, spans, flat = Arrays(), [], []
    for terms in sets:
        flat.append([])
        for array, at, k, span in terms:
            if (k, span) not in spans:
                spans.append((k, span))
            flat[-1].append((known.place(array), at, spans.index((k, span))))
    depth = weight.shape[0] // 4
    operands = list(known.arrays)
    in_specs = [whole_spec(a) for a in operands]
    weights_at = len(operands)
    for k, span in spans:
        if k is None:
            in_specs.append(pl.BlockSpec((depth, tile), lambda n, plan, span=span: (span, n)))
        else:
            in_specs.append(
                pl.BlockSpec((depth * span, tile), lambda n, plan, k=k, span=span: (plan[k] // span, n))
            )
        operands.append(weight)
    totals_at = []
    if total is not None:
        for number in range(len(sets)):
            in_specs.append(pl.BlockSpec((None, rows, tile), lambda n, plan, number=number: (number, 0, n)))
            operands.append(total)
            totals_at.append(len(operands) - 1)
    updating, aliases = None, {}
    if update is None:
        out_shape = jax.ShapeDtypeStruct((len(sets), rows, columns), jnp.float32)
        out_spec = pl.BlockSpec((len(sets), rows, tile), lambda n, plan: (0, 0, n))
    else:
        first_set, shrink, panels = update
        in_specs.append(whole_spec(shrink))
        operands.append(shrink)
        shrink_at, panels_at = len(operands) - 1, []
        for block in range(rows // BLOCK):
            index = PANELS_AT + first_set * (rows // BLOCK) + block
            in_specs.append(
                pl.BlockSpec((None, panels.shape[1], tile), lambda n, plan, index=index: (plan[index], 0, n))
            )
            operands.append(panels)
            panels_at.append(len(operands) - 1)
        updating = (shrink_at, panels_at)
        out_shape = jax.ShapeDtypeStruct(into.shape, into.dtype)
        out_spec = pl.BlockSpec((rows, tile), lambda n, plan: (plan[first_set], n))
        in_specs.append(pl.BlockSpec(memory_space=pl.ANY))
        operands.append(into)
        aliases = {len(operands): 0}
    products = sum(1 if k is None else span for terms in sets for _, _, k, span in terms)
    products *= rows * depth
    moved = 2 * products // rows * columns + 4 * len(sets) * rows * columns * (1 if total is None else 2)
    return pl.pallas_call(
        functools.partial(project_kernel, flat, weights_at, totals_at, updating),
        grid_spec=pltpu.PrefetchScalarGridSpec(
            num_scalar_prefetch=1,
            grid=(columns // tile,),
            in_specs=in_specs,
            out_specs=out_spec,
        ),
        out_shape=out_shape,
        input_output_aliases=aliases,
        cost_estimate=cost(int(weigh * 2 * products * columns), int(weigh * moved)),
        compiler_params=pltpu.CompilerParams(vmem_limit_bytes=VMEM_BYTES),
        name=name,
    )(plan, *operands)


def finish_kernel(count, plan_ref, *refs):
    own_ref, near_ref, panel_one, panel_two, out_ref = refs[0], refs[1], refs[-3], refs[-2], refs[-1]
    number = pl.program_id(0)
    shrink = refs[2][...]
    for other in range(1, count):
        shrink = jnp.where(number == other, refs[2 + other][...], shrink)
    rank = panel_one.shape[0]
    for block, panel in enumerate((panel_one, panel_two)):
        term = adapter_scale * jnp.dot(
            shrink[:, block * rank : (block + 1) * rank], panel[...], preferred_element_type=jnp.float32
        )
        span = slice(block * BLOCK, (block + 1) * BLOCK)

        @pl.when(number == 0)
        def _():
            out_ref[span, :] = (own_ref[span] + term).astype(out_ref.dtype)

        @pl.when(number != 0)
        def _():
            out_ref[span, :] = (near_ref[span] + term).astype(out_ref.dtype)


def finish(own, near, shrinks, panels, plan, row_total):
    _, rows, columns = near.shape
    rank = panels.shape[1]
    tile = tile_of(columns, 2560)
    return pl.pallas_call(
        functools.partial(finish_kernel, 3),
        grid_spec=pltpu.PrefetchScalarGridSpec(
            num_scalar_prefetch=1,
            grid=(3, columns // tile),
            in_specs=[
                pl.BlockSpec((None, rows, tile), lambda s, n, plan: (0, 0, jnp.where(s == 0, n, columns // tile - 1))),
                pl.BlockSpec((None, rows, tile), lambda s, n, plan: (jnp.maximum(s - 1, 0), 0, n)),
            ]
            + [whole_spec(shrink) for shrink in shrinks]
            + [
                pl.BlockSpec(
                    (None, rank, tile), lambda s, n, plan, block=block: (plan[PANELS_AT + 2 * s + block], 0, n)
                )
                for block in range(2)
            ],
            out_specs=pl.BlockSpec((rows, tile), lambda s, n, plan: (plan[s], n)),
        ),
        out_shape=jax.ShapeDtypeStruct((row_total, columns), jnp.bfloat16),
        cost_estimate=cost(12 * rows * rank * columns, 18 * rows * columns),
        compiler_params=pltpu.CompilerParams(vmem_limit_bytes=VMEM_BYTES),
        name="finish_rows",
    )(plan, own, near, *shrinks, panels, panels)


def shrink_kernel(sets, panels_at, plan_ref, *refs):
    panels_ref = refs[panels_at]
    rank = panels_ref.shape[1]
    nt = (((1,), (1,)), ((), ()))
    for number, (terms, out_ref) in enumerate(zip(sets, refs[panels_at + 1 :])):
        blocks = refs[terms[0][0]].shape[-2] // BLOCK
        for block in range(blocks):
            panel = plan_ref[PANELS_AT + number * blocks + block]
            total = 0
            for array, at, start in terms:
                tokens = view(refs[array], at)[block * BLOCK : (block + 1) * BLOCK]
                total += lax.dot_general(
                    tokens,
                    panels_ref[panel, :, start : start + tokens.shape[1]],
                    nt,
                    preferred_element_type=jnp.float32,
                )
            out_ref[:, block * rank : (block + 1) * rank] = total


def shrink_parts(tokens, sets, panels, plan):
    rows, width = tokens.shape
    known = Arrays()
    flat = [[(known.place(tokens), None, 0)]]
    flat += [[(known.place(array), at, start) for array, at, start in terms] for terms in sets]
    operands = known.arrays + [panels]
    _, rank, depth = panels.shape
    shape = (BLOCK, rank * (rows // BLOCK))
    in_specs = [whole_spec(a) for a in operands]
    in_specs[0] = pl.BlockSpec((rows, depth), lambda i, plan: (0, plan[0]))
    return pl.pallas_call(
        functools.partial(shrink_kernel, flat, len(known.arrays)),
        grid_spec=pltpu.PrefetchScalarGridSpec(
            num_scalar_prefetch=1,
            grid=(1,),
            in_specs=in_specs,
            out_specs=[pl.BlockSpec(shape, lambda *_: (0, 0))] * len(flat),
        ),
        out_shape=[jax.ShapeDtypeStruct(shape, jnp.float32)] * len(flat),
        cost_estimate=cost(8 * len(flat) * rows * depth * rank, 2 * (panels.size + len(flat) * rows * depth)),
        compiler_params=pltpu.CompilerParams(vmem_limit_bytes=VMEM_BYTES),
        name="shrink_parts",
    )(plan, *operands)


def after(value, *others):
    return lax.optimization_barrier((value,) + others)[0]


def square(tokens, frozen_weight, down_weight, up_weight, owners, select_slot):
    group = lax.axis_index("grp")
    member = lax.axis_index("tp")
    rows, width = tokens.shape
    blocks = rows // BLOCK
    depth = width // 4
    to_x = lambda v: lax.ppermute(v, "tp", [(i, i ^ 1) for i in range(4)])
    to_y = lambda v: lax.ppermute(v, "tp", [(i, i ^ 2) for i in range(4)])
    across = lambda v: lax.ppermute(v, "tp", [(i, i ^ 3) for i in range(4)])

    members = member ^ jnp.arange(4, dtype=jnp.int32)
    mine = lax.dynamic_slice_in_dim(owners, group * 4 * blocks, 4 * blocks).reshape(4, blocks)
    mine = jnp.sum(jnp.where((members[:, None] == jnp.arange(4))[:, :, None], mine[None], 0), axis=1)
    plan = jnp.concatenate([members, mine.reshape(-1)]).astype(jnp.int32)

    def part(array, start, size):
        return lax.dynamic_slice(array, (0, start), (rows, size))

    def cut(j, *others):
        return part(tokens, after((member ^ 3 ^ j) * depth, *others), depth)

    s0, s3 = cut(0), cut(3)
    x0, y3 = to_x(s0), to_y(s3)
    s1, s2 = cut(1, s0, s3), cut(2, s0, s3)
    x1, y2 = to_x(s1), to_y(s2)
    x2, y1 = to_x(after(s2, x0, y3)), to_y(after(s1, x0, y3))

    def chosen(panels, select):
        return jnp.take(panels, select, axis=0, mode="clip")

    def exchange(panels):
        return lax.all_to_all(panels, "grp", split_axis=0, concat_axis=0, tiled=True)

    down_out = chosen(down_weight, after(select_slot, s1, s2))
    down = exchange(down_out)

    own = project(
        [[(tokens, (i * depth, (i + 1) * depth), None, i) for i in range(4)]],
        frozen_weight, tile_of(frozen_weight.shape[1], 512), after(plan, down_out), rows, weigh=0, name="own_rows",
    )

    tile = tile_of(frozen_weight.shape[1], 512)

    d0, d3 = to_y(after(x0, x1, y2)), to_x(after(y3, x1, y2))
    near = project(
        [[(x0, None, 2, 1), (x1, None, 3, 1)], [(y3, None, 2, 1), (y2, None, 3, 1)]],
        frozen_weight, tile, after(plan, own), rows, weigh=6, name="near_rows",
    )
    up = exchange(chosen(up_weight, after(select_slot, down, near)))
    x3, y0 = to_x(after(s3, x2, y1)), to_y(after(s0, x2, y1))
    near = project(
        [[(x2, None, 0, 1)], [(y1, None, 0, 1)]],
        frozen_weight, tile, plan, rows, total=near, weigh=0, name="near_rows_more",
    )

    share = shrink_parts(tokens, [[(x2, None, 0)], [(y1, None, 0)], [(d0, None, 0)]], down, after(plan, near, d3))
    home = share[0] + to_x(share[1]) + to_y(share[2]) + across(share[3])
    home = home.astype(jnp.bfloat16)
    shrinks = [home, to_x(home), to_y(home), across(home)]
    d1, d2 = to_y(after(x1, home)), to_x(after(y2, home))

    far = project(
        [[(d0, None, 0, 1), (d3, None, 3, 1)]],
        frozen_weight, tile_of(frozen_weight.shape[1], 640), after(plan, share[0]), rows, weigh=4, name="far_rows",
    )
    near = project(
        [[(x3, None, 1, 1)], [(y0, None, 1, 1)]],
        frozen_weight, tile, after(plan, home, far), rows, total=near, weigh=4, name="near_rows_rest",
    )
    out = finish(own, near, shrinks[:3], up, plan, 4 * rows)
    return project(
        [[(d1, None, 1, 1), (d2, None, 2, 1)]],
        frozen_weight, tile_of(frozen_weight.shape[1], 640), plan, rows,
        total=far, update=(3, shrinks[3], up), into=out, name="last_rows",
    )


def general(tokens, frozen_weight, down_weight, up_weight, owners, select_slot):
    tp_count = lax.axis_size("tp")
    group = lax.axis_index("grp")
    member = lax.axis_index("tp")
    local_rows, width = tokens.shape
    group_rows = local_rows * tp_count
    blocks_here = group_rows // BLOCK
    rank_columns = down_weight.shape[1]
    column_slice = up_weight.shape[2]
    my_owners = lax.dynamic_slice_in_dim(owners, group * blocks_here, blocks_here)
    arrived_a, arrived_b = (
        lax.all_to_all(
            jnp.take(panels, select_slot, axis=0), "grp", split_axis=0, concat_axis=0, tiled=True
        )
        for panels in (down_weight, up_weight)
    )
    down_tile = jnp.take(arrived_a, my_owners, axis=0)
    up_tile = jnp.take(arrived_b, my_owners, axis=0)
    whole_a = lax.all_gather(down_tile, "tp", axis=2, tiled=True)
    span_rows = min(local_rows, BLOCK)
    pieces_here = local_rows // span_rows
    first_block = member * local_rows // BLOCK
    local_a = lax.dynamic_slice_in_dim(whole_a, first_block, pieces_here, 0)
    shrink_local = jnp.einsum(
        "pnd,prd->pnr",
        tokens.reshape(pieces_here, span_rows, width),
        local_a,
        preferred_element_type=jnp.float32,
    )
    shrink_local = shrink_local.astype(jnp.bfloat16).reshape(local_rows, rank_columns)
    shrink = lax.all_gather(shrink_local, "tp", axis=0, tiled=True)
    frozen_rows = jnp.dot(
        lax.all_gather(tokens, "tp", axis=0, tiled=True),
        frozen_weight,
        preferred_element_type=jnp.float32,
    )
    update_rows = jnp.einsum(
        "bnr,brc->bnc",
        shrink.reshape(blocks_here, BLOCK, rank_columns),
        up_tile,
        preferred_element_type=jnp.float32,
    )
    update_rows = update_rows.reshape(group_rows, column_slice)
    return (frozen_rows + adapter_scale * update_rows).astype(jnp.bfloat16)


def local(tokens, frozen_weight, down_weight, up_weight, adapter_storage_slot, adapter_of_block):
    group_count = lax.axis_size("grp")
    group = lax.axis_index("grp")
    loaded_here = down_weight.shape[0]
    adapters = jnp.arange(adapter_storage_slot.shape[0])
    named = adapter_of_block[:, None] == adapters[None, :]
    slot_numbers = jnp.sum(jnp.where(named, adapter_storage_slot[None, :], 0), axis=1)
    owners = slot_numbers // loaded_here
    offsets = slot_numbers % loaded_here
    owned_here = owners.reshape(group_count, -1) == group
    select_slot = jnp.sum(jnp.where(owned_here, offsets.reshape(group_count, -1), 0), axis=1)
    fits = lax.axis_size("tp") == 4 and tokens.shape[0] % BLOCK == 0
    way = square if fits else general
    return way(tokens, frozen_weight, down_weight, up_weight, owners, select_slot)


def solution(mesh):
    placed = (
        P(("grp", "tp"), None),
        P(None, "tp"),
        P("grp", None, "tp"),
        P("grp", None, "tp"),
        P(),
        P(),
    )
    return jax.shard_map(
        local, mesh=mesh, in_specs=placed, out_specs=P("grp", "tp"), check_vma=False
    )
```

```python
import functools

import jax
import jax.numpy as jnp
from jax import lax
from jax.experimental import pallas as pl
from jax.experimental.pallas import tpu as pltpu
from jax.sharding import PartitionSpec as P

BLOCK = 128
MIB = 1 << 20
PANELS_AT = 4
VMEM_BYTES = 24 * MIB

adapter_scale = 0.5


def tile_of(columns, most):
    return max(t for t in range(128, most + 1, 128) if columns % t == 0)


def whole_spec(array):
    zeros = (0,) * array.ndim
    return pl.BlockSpec(array.shape, lambda *_: zeros)


def cost(flops, moved):
    return pl.CostEstimate(flops=flops, bytes_accessed=moved, transcendentals=0)


class Arrays:
    def __init__(self):
        self.arrays = []

    def place(self, array):
        for number, known in enumerate(self.arrays):
            if known is array:
                return number
        self.arrays.append(array)
        return len(self.arrays) - 1


def view(ref, at):
    if at is None:
        return ref[...]
    return ref[:, at[0] : at[1]] if isinstance(at, tuple) else ref[at]


def project_kernel(sets, weights_at, totals_at, update, plan_ref, *refs):
    out_ref = refs[-1]
    for number, terms in enumerate(sets):
        total = None
        for array, at, weight in terms:
            part = jnp.dot(
                view(refs[array], at), refs[weights_at + weight][...], preferred_element_type=jnp.float32
            )
            total = part if total is None else total + part
        if totals_at:
            before = refs[totals_at[number]][...]
            total = before if total is None else total + before
        if update is None:
            out_ref[number] = total
        else:
            shrink_at, panels_at = update
            shrink = refs[shrink_at][...]
            for block, panel in enumerate(panels_at):
                rank = refs[panel].shape[0]
                term = jnp.dot(
                    shrink[:, block * rank : (block + 1) * rank],
                    refs[panel][...],
                    preferred_element_type=jnp.float32,
                )
                span = slice(block * BLOCK, (block + 1) * BLOCK)
                out_ref[span, :] = (total[span] + adapter_scale * term).astype(out_ref.dtype)


def project(sets, weight, tile, plan, rows, total=None, update=None, into=None, weigh=2, name=None):
    columns = weight.shape[1]
    known, spans, flat = Arrays(), [], []
    for terms in sets:
        flat.append([])
        for array, at, k, span in terms:
            if (k, span) not in spans:
                spans.append((k, span))
            flat[-1].append((known.place(array), at, spans.index((k, span))))
    depth = weight.shape[0] // 4
    operands = list(known.arrays)
    in_specs = [whole_spec(a) for a in operands]
    weights_at = len(operands)
    for k, span in spans:
        if k is None:
            in_specs.append(pl.BlockSpec((depth, tile), lambda n, plan, span=span: (span, n)))
        else:
            in_specs.append(
                pl.BlockSpec((depth * span, tile), lambda n, plan, k=k, span=span: (plan[k] // span, n))
            )
        operands.append(weight)
    totals_at = []
    if total is not None:
        total = pltpu.with_memory_space_constraint(total, pltpu.HBM)
        for number in range(len(sets)):
            in_specs.append(pl.BlockSpec((None, rows, tile), lambda n, plan, number=number: (number, 0, n)))
            operands.append(total)
            totals_at.append(len(operands) - 1)
    updating, aliases = None, {}
    if update is None:
        out_shape = pltpu.HBM((len(sets), rows, columns), jnp.float32)
        out_spec = pl.BlockSpec((len(sets), rows, tile), lambda n, plan: (0, 0, n))
    else:
        first_set, shrink, panels = update
        panels = pltpu.with_memory_space_constraint(panels, pltpu.HBM)
        in_specs.append(whole_spec(shrink))
        operands.append(shrink)
        shrink_at, panels_at = len(operands) - 1, []
        for block in range(rows // BLOCK):
            index = PANELS_AT + first_set * (rows // BLOCK) + block
            in_specs.append(
                pl.BlockSpec((None, panels.shape[1], tile), lambda n, plan, index=index: (plan[index], 0, n))
            )
            operands.append(panels)
            panels_at.append(len(operands) - 1)
        updating = (shrink_at, panels_at)
        out_shape = jax.ShapeDtypeStruct(into.shape, into.dtype)
        out_spec = pl.BlockSpec((rows, tile), lambda n, plan: (plan[first_set], n))
        in_specs.append(pl.BlockSpec(memory_space=pl.ANY))
        operands.append(into)
        aliases = {len(operands): 0}
    products = sum(1 if k is None else span for terms in sets for _, _, k, span in terms)
    products *= rows * depth
    moved = 2 * products // rows * columns + 4 * len(sets) * rows * columns * (1 if total is None else 2)
    return pl.pallas_call(
        functools.partial(project_kernel, flat, weights_at, totals_at, updating),
        grid_spec=pltpu.PrefetchScalarGridSpec(
            num_scalar_prefetch=1,
            grid=(columns // tile,),
            in_specs=in_specs,
            out_specs=out_spec,
        ),
        out_shape=out_shape,
        input_output_aliases=aliases,
        cost_estimate=cost(int(weigh * 2 * products * columns), int(weigh * moved)),
        compiler_params=pltpu.CompilerParams(vmem_limit_bytes=VMEM_BYTES),
        name=name,
    )(plan, *operands)


def finish_kernel(count, plan_ref, *refs):
    own_ref, near_ref, panel_one, panel_two, out_ref = refs[0], refs[1], refs[-3], refs[-2], refs[-1]
    number = pl.program_id(0)
    shrink = refs[2][...]
    for other in range(1, count):
        shrink = jnp.where(number == other, refs[2 + other][...], shrink)
    rank = panel_one.shape[0]
    for block, panel in enumerate((panel_one, panel_two)):
        term = adapter_scale * jnp.dot(
            shrink[:, block * rank : (block + 1) * rank], panel[...], preferred_element_type=jnp.float32
        )
        span = slice(block * BLOCK, (block + 1) * BLOCK)

        @pl.when(number == 0)
        def _():
            out_ref[span, :] = (own_ref[span] + term).astype(out_ref.dtype)

        @pl.when(number != 0)
        def _():
            out_ref[span, :] = (near_ref[span] + term).astype(out_ref.dtype)


def finish(own, near, shrinks, panels, plan, row_total):
    _, rows, columns = near.shape
    rank = panels.shape[1]
    own, near, panels = (pltpu.with_memory_space_constraint(array, pltpu.HBM) for array in (own, near, panels))
    tile = tile_of(columns, 2560)
    return pl.pallas_call(
        functools.partial(finish_kernel, 3),
        grid_spec=pltpu.PrefetchScalarGridSpec(
            num_scalar_prefetch=1,
            grid=(3, columns // tile),
            in_specs=[
                pl.BlockSpec((None, rows, tile), lambda s, n, plan: (0, 0, jnp.where(s == 0, n, columns // tile - 1))),
                pl.BlockSpec((None, rows, tile), lambda s, n, plan: (jnp.maximum(s - 1, 0), 0, n)),
            ]
            + [whole_spec(shrink) for shrink in shrinks]
            + [
                pl.BlockSpec(
                    (None, rank, tile), lambda s, n, plan, block=block: (plan[PANELS_AT + 2 * s + block], 0, n)
                )
                for block in range(2)
            ],
            out_specs=pl.BlockSpec((rows, tile), lambda s, n, plan: (plan[s], n)),
        ),
        out_shape=jax.ShapeDtypeStruct((row_total, columns), jnp.bfloat16),
        cost_estimate=cost(12 * rows * rank * columns, 18 * rows * columns),
        compiler_params=pltpu.CompilerParams(vmem_limit_bytes=VMEM_BYTES),
        name="finish_rows",
    )(plan, own, near, *shrinks, panels, panels)


def shrink_kernel(sets, panels_at, plan_ref, *refs):
    panels_ref = refs[panels_at]
    rank = panels_ref.shape[1]
    nt = (((1,), (1,)), ((), ()))
    for number, (terms, out_ref) in enumerate(zip(sets, refs[panels_at + 1 :])):
        blocks = refs[terms[0][0]].shape[-2] // BLOCK
        for block in range(blocks):
            panel = plan_ref[PANELS_AT + number * blocks + block]
            total = 0
            for array, at, start in terms:
                tokens = view(refs[array], at)[block * BLOCK : (block + 1) * BLOCK]
                total += lax.dot_general(
                    tokens,
                    panels_ref[panel, :, start : start + tokens.shape[1]],
                    nt,
                    preferred_element_type=jnp.float32,
                )
            out_ref[:, block * rank : (block + 1) * rank] = total


def shrink_parts(tokens, sets, panels, plan):
    rows, width = tokens.shape
    known = Arrays()
    flat = [[(known.place(tokens), None, 0)]]
    flat += [[(known.place(array), at, start) for array, at, start in terms] for terms in sets]
    operands = known.arrays + [panels]
    _, rank, depth = panels.shape
    shape = (BLOCK, rank * (rows // BLOCK))
    in_specs = [whole_spec(a) for a in operands]
    in_specs[0] = pl.BlockSpec((rows, depth), lambda i, plan: (0, plan[0]))
    return pl.pallas_call(
        functools.partial(shrink_kernel, flat, len(known.arrays)),
        grid_spec=pltpu.PrefetchScalarGridSpec(
            num_scalar_prefetch=1,
            grid=(1,),
            in_specs=in_specs,
            out_specs=[pl.BlockSpec(shape, lambda *_: (0, 0))] * len(flat),
        ),
        out_shape=[jax.ShapeDtypeStruct(shape, jnp.float32)] * len(flat),
        cost_estimate=cost(8 * len(flat) * rows * depth * rank, 2 * (panels.size + len(flat) * rows * depth)),
        compiler_params=pltpu.CompilerParams(vmem_limit_bytes=VMEM_BYTES),
        name="shrink_parts",
    )(plan, *operands)


def after(value, *others):
    return lax.optimization_barrier((value,) + others)[0]


def square(tokens, frozen_weight, down_weight, up_weight, owners, select_slot):
    group = lax.axis_index("grp")
    member = lax.axis_index("tp")
    rows, width = tokens.shape
    blocks = rows // BLOCK
    depth = width // 4
    to_x = lambda v: lax.ppermute(v, "tp", [(i, i ^ 1) for i in range(4)])
    to_y = lambda v: lax.ppermute(v, "tp", [(i, i ^ 2) for i in range(4)])
    across = lambda v: lax.ppermute(v, "tp", [(i, i ^ 3) for i in range(4)])

    members = member ^ jnp.arange(4, dtype=jnp.int32)
    mine = lax.dynamic_slice_in_dim(owners, group * 4 * blocks, 4 * blocks).reshape(4, blocks)
    mine = jnp.sum(jnp.where((members[:, None] == jnp.arange(4))[:, :, None], mine[None], 0), axis=1)
    plan = jnp.concatenate([members, mine.reshape(-1)]).astype(jnp.int32)

    def part(array, start, size):
        return lax.dynamic_slice(array, (0, start), (rows, size))

    def cut(j, *others):
        return part(tokens, after((member ^ 3 ^ j) * depth, *others), depth)

    s0, s3 = cut(0), cut(3)
    x0, y3 = to_x(s0), to_y(s3)
    s1, s2 = cut(1, s0, s3), cut(2, s0, s3)
    x1, y2 = to_x(s1), to_y(s2)
    x2, y1 = to_x(after(s2, x0, y3)), to_y(after(s1, x0, y3))

    def chosen(panels, select):
        return jnp.take(panels, select, axis=0, mode="clip")

    def exchange(panels):
        return lax.all_to_all(panels, "grp", split_axis=0, concat_axis=0, tiled=True)

    down_out = chosen(down_weight, after(select_slot, s0, s3))
    down = exchange(down_out)

    own = project(
        [[(tokens, (i * depth, (i + 1) * depth), None, i) for i in range(4)]],
        frozen_weight, tile_of(frozen_weight.shape[1], 256), after(plan, down_out), rows, weigh=0, name="own_rows",
    )

    tile = tile_of(frozen_weight.shape[1], 512)

    d0, d3 = to_y(after(x0, x1, y2)), to_x(after(y3, x1, y2))
    near = project(
        [[(x0, None, 2, 1), (x1, None, 3, 1)], [(y3, None, 2, 1), (y2, None, 3, 1)]],
        frozen_weight, tile, after(plan, own), rows, weigh=6, name="near_rows",
    )
    up = exchange(chosen(up_weight, after(select_slot, down, near)))
    x3, y0 = to_x(after(s3, x2, y1)), to_y(after(s0, x2, y1))
    near = project(
        [[(x2, None, 0, 1)], [(y1, None, 0, 1)]],
        frozen_weight, tile, plan, rows, total=near, weigh=0, name="near_rows_more",
    )

    share = shrink_parts(tokens, [[(x2, None, 0)], [(y1, None, 0)], [(d0, None, 0)]], down, after(plan, near, d3))
    home = share[0] + to_x(share[1]) + to_y(share[2]) + across(share[3])
    home = home.astype(jnp.bfloat16)
    shrinks = [home, to_x(home), to_y(home), across(home)]
    d1, d2 = to_y(after(x1, home)), to_x(after(y2, home))

    far = project(
        [[(d0, None, 0, 1), (d3, None, 3, 1)]],
        frozen_weight, tile_of(frozen_weight.shape[1], 640), after(plan, share[0]), rows, weigh=4, name="far_rows",
    )
    near = project(
        [[(x3, None, 1, 1)], [(y0, None, 1, 1)]],
        frozen_weight, tile, after(plan, home, far), rows, total=near, weigh=4, name="near_rows_rest",
    )
    out = finish(own, near, shrinks[:3], up, plan, 4 * rows)
    return project(
        [[(d1, None, 1, 1), (d2, None, 2, 1)]],
        frozen_weight, tile_of(frozen_weight.shape[1], 640), plan, rows,
        total=far, update=(3, shrinks[3], up), into=out, name="last_rows",
    )


def general(tokens, frozen_weight, down_weight, up_weight, owners, select_slot):
    tp_count = lax.axis_size("tp")
    group = lax.axis_index("grp")
    member = lax.axis_index("tp")
    local_rows, width = tokens.shape
    group_rows = local_rows * tp_count
    blocks_here = group_rows // BLOCK
    rank_columns = down_weight.shape[1]
    column_slice = up_weight.shape[2]
    my_owners = lax.dynamic_slice_in_dim(owners, group * blocks_here, blocks_here)
    arrived_a, arrived_b = (
        lax.all_to_all(
            jnp.take(panels, select_slot, axis=0), "grp", split_axis=0, concat_axis=0, tiled=True
        )
        for panels in (down_weight, up_weight)
    )
    down_tile = jnp.take(arrived_a, my_owners, axis=0)
    up_tile = jnp.take(arrived_b, my_owners, axis=0)
    whole_a = lax.all_gather(down_tile, "tp", axis=2, tiled=True)
    span_rows = min(local_rows, BLOCK)
    pieces_here = local_rows // span_rows
    first_block = member * local_rows // BLOCK
    local_a = lax.dynamic_slice_in_dim(whole_a, first_block, pieces_here, 0)
    shrink_local = jnp.einsum(
        "pnd,prd->pnr",
        tokens.reshape(pieces_here, span_rows, width),
        local_a,
        preferred_element_type=jnp.float32,
    )
    shrink_local = shrink_local.astype(jnp.bfloat16).reshape(local_rows, rank_columns)
    shrink = lax.all_gather(shrink_local, "tp", axis=0, tiled=True)
    frozen_rows = jnp.dot(
        lax.all_gather(tokens, "tp", axis=0, tiled=True),
        frozen_weight,
        preferred_element_type=jnp.float32,
    )
    update_rows = jnp.einsum(
        "bnr,brc->bnc",
        shrink.reshape(blocks_here, BLOCK, rank_columns),
        up_tile,
        preferred_element_type=jnp.float32,
    )
    update_rows = update_rows.reshape(group_rows, column_slice)
    return (frozen_rows + adapter_scale * update_rows).astype(jnp.bfloat16)


def local(tokens, frozen_weight, down_weight, up_weight, adapter_storage_slot, adapter_of_block):
    group_count = lax.axis_size("grp")
    group = lax.axis_index("grp")
    loaded_here = down_weight.shape[0]
    adapters = jnp.arange(adapter_storage_slot.shape[0])
    named = adapter_of_block[:, None] == adapters[None, :]
    slot_numbers = jnp.sum(jnp.where(named, adapter_storage_slot[None, :], 0), axis=1)
    owners = slot_numbers // loaded_here
    offsets = slot_numbers % loaded_here
    owned_here = owners.reshape(group_count, -1) == group
    select_slot = jnp.sum(jnp.where(owned_here, offsets.reshape(group_count, -1), 0), axis=1)
    fits = lax.axis_size("tp") == 4 and tokens.shape[0] % BLOCK == 0
    way = square if fits else general
    return way(tokens, frozen_weight, down_weight, up_weight, owners, select_slot)


def solution(mesh):
    placed = (
        P(("grp", "tp"), None),
        P(None, "tp"),
        P("grp", None, "tp"),
        P("grp", None, "tp"),
        P(),
        P(),
    )
    return jax.shard_map(
        local, mesh=mesh, in_specs=placed, out_specs=P("grp", "tp"), check_vma=False
    )
```

```python
import functools

import jax
import jax.numpy as jnp
from jax import lax
from jax.experimental import pallas as pl
from jax.experimental.pallas import tpu as pltpu
from jax.sharding import PartitionSpec as P

BLOCK = 128
MIB = 1 << 20
PANELS_AT = 4
VMEM_BYTES = 24 * MIB

adapter_scale = 0.5


def tile_of(columns, most):
    return max(t for t in range(128, most + 1, 128) if columns % t == 0)


def whole_spec(array):
    zeros = (0,) * array.ndim
    return pl.BlockSpec(array.shape, lambda *_: zeros)


def cost(flops, moved):
    return pl.CostEstimate(flops=flops, bytes_accessed=moved, transcendentals=0)


class Arrays:
    def __init__(self):
        self.arrays = []

    def place(self, array):
        for number, known in enumerate(self.arrays):
            if known is array:
                return number
        self.arrays.append(array)
        return len(self.arrays) - 1


def view(ref, at):
    if at is None:
        return ref[...]
    return ref[:, at[0] : at[1]] if isinstance(at, tuple) else ref[at]


def cut_kernel(member_ref, tokens_ref, far_ref, own_ref, sems):
    depth = far_ref.shape[1]
    copies = []
    for number, (out_ref, flip) in enumerate(((far_ref, 3), (own_ref, 0))):
        start = pl.multiple_of((member_ref[0] ^ flip) * depth, depth)
        copies.append(pltpu.make_async_copy(tokens_ref.at[:, pl.ds(start, depth)], out_ref, sems.at[number]))
    for copy in copies:
        copy.start()
    for copy in copies:
        copy.wait()


def first_cuts(tokens, member):
    rows, width = tokens.shape
    shape = (rows, width // 4)
    return pl.pallas_call(
        cut_kernel,
        grid_spec=pltpu.PrefetchScalarGridSpec(
            num_scalar_prefetch=1,
            grid=(1,),
            in_specs=[pl.BlockSpec(memory_space=pl.ANY)],
            out_specs=[pl.BlockSpec(memory_space=pltpu.VMEM)] * 2,
            scratch_shapes=[pltpu.SemaphoreType.DMA((2,))],
        ),
        out_shape=[pltpu.VMEM(shape, tokens.dtype)] * 2,
        cost_estimate=cost(0, 2 * tokens.size),
        name="first_cuts",
    )(member.astype(jnp.int32).reshape(1), tokens)


def project_kernel(sets, weights_at, totals_at, update, plan_ref, *refs):
    out_ref = refs[-1]
    for number, terms in enumerate(sets):
        total = None
        for array, at, weight in terms:
            part = jnp.dot(
                view(refs[array], at), refs[weights_at + weight][...], preferred_element_type=jnp.float32
            )
            total = part if total is None else total + part
        if totals_at:
            before = refs[totals_at[number]][...]
            total = before if total is None else total + before
        if update is None:
            out_ref[number] = total
        else:
            shrink_at, panels_at = update
            shrink = refs[shrink_at][...]
            for block, panel in enumerate(panels_at):
                rank = refs[panel].shape[0]
                term = jnp.dot(
                    shrink[:, block * rank : (block + 1) * rank],
                    refs[panel][...],
                    preferred_element_type=jnp.float32,
                )
                span = slice(block * BLOCK, (block + 1) * BLOCK)
                out_ref[span, :] = (total[span] + adapter_scale * term).astype(out_ref.dtype)


def project(sets, weight, tile, plan, rows, total=None, update=None, into=None, weigh=2, name=None):
    columns = weight.shape[1]
    known, spans, flat = Arrays(), [], []
    for terms in sets:
        flat.append([])
        for array, at, k, span in terms:
            if (k, span) not in spans:
                spans.append((k, span))
            flat[-1].append((known.place(array), at, spans.index((k, span))))
    depth = weight.shape[0] // 4
    operands = list(known.arrays)
    in_specs = [whole_spec(a) for a in operands]
    weights_at = len(operands)
    for k, span in spans:
        if k is None:
            in_specs.append(pl.BlockSpec((depth, tile), lambda n, plan, span=span: (span, n)))
        else:
            in_specs.append(
                pl.BlockSpec((depth * span, tile), lambda n, plan, k=k, span=span: (plan[k] // span, n))
            )
        operands.append(weight)
    totals_at = []
    if total is not None:
        total = pltpu.with_memory_space_constraint(total, pltpu.HBM)
        for number in range(len(sets)):
            in_specs.append(pl.BlockSpec((None, rows, tile), lambda n, plan, number=number: (number, 0, n)))
            operands.append(total)
            totals_at.append(len(operands) - 1)
    updating, aliases = None, {}
    if update is None:
        out_shape = pltpu.HBM((len(sets), rows, columns), jnp.float32)
        out_spec = pl.BlockSpec((len(sets), rows, tile), lambda n, plan: (0, 0, n))
    else:
        first_set, shrink, panels = update
        panels = pltpu.with_memory_space_constraint(panels, pltpu.HBM)
        in_specs.append(whole_spec(shrink))
        operands.append(shrink)
        shrink_at, panels_at = len(operands) - 1, []
        for block in range(rows // BLOCK):
            index = PANELS_AT + first_set * (rows // BLOCK) + block
            in_specs.append(
                pl.BlockSpec((None, panels.shape[1], tile), lambda n, plan, index=index: (plan[index], 0, n))
            )
            operands.append(panels)
            panels_at.append(len(operands) - 1)
        updating = (shrink_at, panels_at)
        out_shape = jax.ShapeDtypeStruct(into.shape, into.dtype)
        out_spec = pl.BlockSpec((rows, tile), lambda n, plan: (plan[first_set], n))
        in_specs.append(pl.BlockSpec(memory_space=pl.ANY))
        operands.append(into)
        aliases = {len(operands): 0}
    products = sum(1 if k is None else span for terms in sets for _, _, k, span in terms)
    products *= rows * depth
    moved = 2 * products // rows * columns + 4 * len(sets) * rows * columns * (1 if total is None else 2)
    return pl.pallas_call(
        functools.partial(project_kernel, flat, weights_at, totals_at, updating),
        grid_spec=pltpu.PrefetchScalarGridSpec(
            num_scalar_prefetch=1,
            grid=(columns // tile,),
            in_specs=in_specs,
            out_specs=out_spec,
        ),
        out_shape=out_shape,
        input_output_aliases=aliases,
        cost_estimate=cost(int(weigh * 2 * products * columns), int(weigh * moved)),
        compiler_params=pltpu.CompilerParams(vmem_limit_bytes=VMEM_BYTES),
        name=name,
    )(plan, *operands)


def finish_kernel(count, plan_ref, *refs):
    own_ref, near_ref, panel_one, panel_two, out_ref = refs[0], refs[1], refs[-3], refs[-2], refs[-1]
    number = pl.program_id(0)
    shrink = refs[2][...]
    for other in range(1, count):
        shrink = jnp.where(number == other, refs[2 + other][...], shrink)
    rank = panel_one.shape[0]
    for block, panel in enumerate((panel_one, panel_two)):
        term = adapter_scale * jnp.dot(
            shrink[:, block * rank : (block + 1) * rank], panel[...], preferred_element_type=jnp.float32
        )
        span = slice(block * BLOCK, (block + 1) * BLOCK)

        @pl.when(number == 0)
        def _():
            out_ref[span, :] = (own_ref[span] + term).astype(out_ref.dtype)

        @pl.when(number != 0)
        def _():
            out_ref[span, :] = (near_ref[span] + term).astype(out_ref.dtype)


def finish(own, near, shrinks, panels, plan, row_total):
    _, rows, columns = near.shape
    rank = panels.shape[1]
    own, near, panels = (pltpu.with_memory_space_constraint(array, pltpu.HBM) for array in (own, near, panels))
    tile = tile_of(columns, 2560)
    return pl.pallas_call(
        functools.partial(finish_kernel, 3),
        grid_spec=pltpu.PrefetchScalarGridSpec(
            num_scalar_prefetch=1,
            grid=(3, columns // tile),
            in_specs=[
                pl.BlockSpec((None, rows, tile), lambda s, n, plan: (0, 0, jnp.where(s == 0, n, columns // tile - 1))),
                pl.BlockSpec((None, rows, tile), lambda s, n, plan: (jnp.maximum(s - 1, 0), 0, n)),
            ]
            + [whole_spec(shrink) for shrink in shrinks]
            + [
                pl.BlockSpec(
                    (None, rank, tile), lambda s, n, plan, block=block: (plan[PANELS_AT + 2 * s + block], 0, n)
                )
                for block in range(2)
            ],
            out_specs=pl.BlockSpec((rows, tile), lambda s, n, plan: (plan[s], n)),
        ),
        out_shape=jax.ShapeDtypeStruct((row_total, columns), jnp.bfloat16),
        cost_estimate=cost(12 * rows * rank * columns, 18 * rows * columns),
        compiler_params=pltpu.CompilerParams(vmem_limit_bytes=VMEM_BYTES),
        name="finish_rows",
    )(plan, own, near, *shrinks, panels, panels)


def shrink_kernel(sets, panels_at, plan_ref, *refs):
    panels_ref = refs[panels_at]
    rank = panels_ref.shape[1]
    nt = (((1,), (1,)), ((), ()))
    for number, (terms, out_ref) in enumerate(zip(sets, refs[panels_at + 1 :])):
        blocks = refs[terms[0][0]].shape[-2] // BLOCK
        for block in range(blocks):
            panel = plan_ref[PANELS_AT + number * blocks + block]
            total = 0
            for array, at, start in terms:
                tokens = view(refs[array], at)[block * BLOCK : (block + 1) * BLOCK]
                total += lax.dot_general(
                    tokens,
                    panels_ref[panel, :, start : start + tokens.shape[1]],
                    nt,
                    preferred_element_type=jnp.float32,
                )
            out_ref[:, block * rank : (block + 1) * rank] = total


def shrink_parts(tokens, sets, panels, plan):
    rows, width = tokens.shape
    known = Arrays()
    flat = [[(known.place(tokens), None, 0)]]
    flat += [[(known.place(array), at, start) for array, at, start in terms] for terms in sets]
    operands = known.arrays + [panels]
    _, rank, depth = panels.shape
    shape = (BLOCK, rank * (rows // BLOCK))
    in_specs = [whole_spec(a) for a in operands]
    in_specs[0] = pl.BlockSpec((rows, depth), lambda i, plan: (0, plan[0]))
    return pl.pallas_call(
        functools.partial(shrink_kernel, flat, len(known.arrays)),
        grid_spec=pltpu.PrefetchScalarGridSpec(
            num_scalar_prefetch=1,
            grid=(1,),
            in_specs=in_specs,
            out_specs=[pl.BlockSpec(shape, lambda *_: (0, 0))] * len(flat),
        ),
        out_shape=[jax.ShapeDtypeStruct(shape, jnp.float32)] * len(flat),
        cost_estimate=cost(8 * len(flat) * rows * depth * rank, 2 * (panels.size + len(flat) * rows * depth)),
        compiler_params=pltpu.CompilerParams(vmem_limit_bytes=VMEM_BYTES),
        name="shrink_parts",
    )(plan, *operands)


def after(value, *others):
    return lax.optimization_barrier((value,) + others)[0]


def square(tokens, frozen_weight, down_weight, up_weight, owners, select_slot):
    group = lax.axis_index("grp")
    member = lax.axis_index("tp")
    rows, width = tokens.shape
    blocks = rows // BLOCK
    depth = width // 4
    to_x = lambda v: lax.ppermute(v, "tp", [(i, i ^ 1) for i in range(4)])
    to_y = lambda v: lax.ppermute(v, "tp", [(i, i ^ 2) for i in range(4)])
    across = lambda v: lax.ppermute(v, "tp", [(i, i ^ 3) for i in range(4)])

    members = member ^ jnp.arange(4, dtype=jnp.int32)
    mine = lax.dynamic_slice_in_dim(owners, group * 4 * blocks, 4 * blocks).reshape(4, blocks)
    mine = jnp.sum(jnp.where((members[:, None] == jnp.arange(4))[:, :, None], mine[None], 0), axis=1)
    plan = jnp.concatenate([members, mine.reshape(-1)]).astype(jnp.int32)

    def part(array, start, size):
        return lax.dynamic_slice(array, (0, start), (rows, size))

    def cut(j, *others):
        return part(tokens, after((member ^ 3 ^ j) * depth, *others), depth)

    s0, s3 = first_cuts(tokens, member)
    x0, y3 = to_x(s0), to_y(s3)
    s1, s2 = cut(1, s0, s3), cut(2, s0, s3)
    x1, y2 = to_x(s1), to_y(s2)
    x2, y1 = to_x(after(s2, x0, y3)), to_y(after(s1, x0, y3))

    def chosen(panels, select):
        return jnp.take(panels, select, axis=0, mode="clip")

    def exchange(panels):
        return lax.all_to_all(panels, "grp", split_axis=0, concat_axis=0, tiled=True)

    down_out = chosen(down_weight, after(select_slot, s0, s3))
    down = exchange(down_out)

    own = project(
        [[(tokens, (i * depth, (i + 1) * depth), None, i) for i in range(4)]],
        frozen_weight, tile_of(frozen_weight.shape[1], 256), after(plan, down_out), rows, weigh=0, name="own_rows",
    )

    tile = tile_of(frozen_weight.shape[1], 512)

    d0, d3 = to_y(after(x0, x1, y2)), to_x(after(y3, x1, y2))
    near = project(
        [[(x0, None, 2, 1), (x1, None, 3, 1)], [(y3, None, 2, 1), (y2, None, 3, 1)]],
        frozen_weight, tile, after(plan, own), rows, weigh=6, name="near_rows",
    )
    up = exchange(chosen(up_weight, after(select_slot, down, near)))
    x3, y0 = to_x(after(s3, x2, y1)), to_y(after(s0, x2, y1))
    near = project(
        [[(x2, None, 0, 1)], [(y1, None, 0, 1)]],
        frozen_weight, tile, plan, rows, total=near, weigh=0, name="near_rows_more",
    )

    share = shrink_parts(tokens, [[(x2, None, 0)], [(y1, None, 0)], [(d0, None, 0)]], down, after(plan, near, d3))
    home = share[0] + to_x(share[1]) + to_y(share[2]) + across(share[3])
    home = home.astype(jnp.bfloat16)
    shrinks = [home, to_x(home), to_y(home), across(home)]
    d1, d2 = to_y(after(x1, home)), to_x(after(y2, home))

    far = project(
        [[(d0, None, 0, 1), (d3, None, 3, 1)]],
        frozen_weight, tile_of(frozen_weight.shape[1], 640), after(plan, share[0]), rows, weigh=4, name="far_rows",
    )
    near = project(
        [[(x3, None, 1, 1)], [(y0, None, 1, 1)]],
        frozen_weight, tile, after(plan, home, far), rows, total=near, weigh=4, name="near_rows_rest",
    )
    out = finish(own, near, shrinks[:3], up, plan, 4 * rows)
    return project(
        [[(d1, None, 1, 1), (d2, None, 2, 1)]],
        frozen_weight, tile_of(frozen_weight.shape[1], 640), plan, rows,
        total=far, update=(3, shrinks[3], up), into=out, name="last_rows",
    )


def general(tokens, frozen_weight, down_weight, up_weight, owners, select_slot):
    tp_count = lax.axis_size("tp")
    group = lax.axis_index("grp")
    member = lax.axis_index("tp")
    local_rows, width = tokens.shape
    group_rows = local_rows * tp_count
    blocks_here = group_rows // BLOCK
    rank_columns = down_weight.shape[1]
    column_slice = up_weight.shape[2]
    my_owners = lax.dynamic_slice_in_dim(owners, group * blocks_here, blocks_here)
    arrived_a, arrived_b = (
        lax.all_to_all(
            jnp.take(panels, select_slot, axis=0), "grp", split_axis=0, concat_axis=0, tiled=True
        )
        for panels in (down_weight, up_weight)
    )
    down_tile = jnp.take(arrived_a, my_owners, axis=0)
    up_tile = jnp.take(arrived_b, my_owners, axis=0)
    whole_a = lax.all_gather(down_tile, "tp", axis=2, tiled=True)
    span_rows = min(local_rows, BLOCK)
    pieces_here = local_rows // span_rows
    first_block = member * local_rows // BLOCK
    local_a = lax.dynamic_slice_in_dim(whole_a, first_block, pieces_here, 0)
    shrink_local = jnp.einsum(
        "pnd,prd->pnr",
        tokens.reshape(pieces_here, span_rows, width),
        local_a,
        preferred_element_type=jnp.float32,
    )
    shrink_local = shrink_local.astype(jnp.bfloat16).reshape(local_rows, rank_columns)
    shrink = lax.all_gather(shrink_local, "tp", axis=0, tiled=True)
    frozen_rows = jnp.dot(
        lax.all_gather(tokens, "tp", axis=0, tiled=True),
        frozen_weight,
        preferred_element_type=jnp.float32,
    )
    update_rows = jnp.einsum(
        "bnr,brc->bnc",
        shrink.reshape(blocks_here, BLOCK, rank_columns),
        up_tile,
        preferred_element_type=jnp.float32,
    )
    update_rows = update_rows.reshape(group_rows, column_slice)
    return (frozen_rows + adapter_scale * update_rows).astype(jnp.bfloat16)


def local(tokens, frozen_weight, down_weight, up_weight, adapter_storage_slot, adapter_of_block):
    group_count = lax.axis_size("grp")
    group = lax.axis_index("grp")
    loaded_here = down_weight.shape[0]
    adapters = jnp.arange(adapter_storage_slot.shape[0])
    named = adapter_of_block[:, None] == adapters[None, :]
    slot_numbers = jnp.sum(jnp.where(named, adapter_storage_slot[None, :], 0), axis=1)
    owners = slot_numbers // loaded_here
    offsets = slot_numbers % loaded_here
    owned_here = owners.reshape(group_count, -1) == group
    select_slot = jnp.sum(jnp.where(owned_here, offsets.reshape(group_count, -1), 0), axis=1)
    fits = lax.axis_size("tp") == 4 and tokens.shape[0] % BLOCK == 0
    way = square if fits else general
    return way(tokens, frozen_weight, down_weight, up_weight, owners, select_slot)


def solution(mesh):
    placed = (
        P(("grp", "tp"), None),
        P(None, "tp"),
        P("grp", None, "tp"),
        P("grp", None, "tp"),
        P(),
        P(),
    )
    return jax.shard_map(
        local, mesh=mesh, in_specs=placed, out_specs=P("grp", "tp"), check_vma=False
    )
```

```python
import functools

import jax
import jax.numpy as jnp
from jax import lax
from jax.experimental import pallas as pl
from jax.experimental.pallas import tpu as pltpu
from jax.sharding import PartitionSpec as P

BLOCK = 128
MIB = 1 << 20
PANELS_AT = 4
VMEM_BYTES = 24 * MIB

adapter_scale = 0.5


def tile_of(columns, most):
    return max(t for t in range(128, most + 1, 128) if columns % t == 0)


def whole_spec(array):
    zeros = (0,) * array.ndim
    return pl.BlockSpec(array.shape, lambda *_: zeros)


def cost(flops, moved):
    return pl.CostEstimate(flops=flops, bytes_accessed=moved, transcendentals=0)


class Arrays:
    def __init__(self):
        self.arrays = []

    def place(self, array):
        for number, known in enumerate(self.arrays):
            if known is array:
                return number
        self.arrays.append(array)
        return len(self.arrays) - 1


def view(ref, at):
    return ref[...] if at is None else ref[:, at[0] : at[1]]


def cut_kernel(member_ref, tokens_ref, far_ref, own_ref, sems):
    depth = far_ref.shape[1]
    copies = []
    for number, (out_ref, flip) in enumerate(((far_ref, 3), (own_ref, 0))):
        start = pl.multiple_of((member_ref[0] ^ flip) * depth, depth)
        copies.append(pltpu.make_async_copy(tokens_ref.at[:, pl.ds(start, depth)], out_ref, sems.at[number]))
    for copy in copies:
        copy.start()
    for copy in copies:
        copy.wait()


def first_cuts(tokens, member):
    rows, width = tokens.shape
    shape = (rows, width // 4)
    return pl.pallas_call(
        cut_kernel,
        grid_spec=pltpu.PrefetchScalarGridSpec(
            num_scalar_prefetch=1,
            grid=(1,),
            in_specs=[pl.BlockSpec(memory_space=pl.ANY)],
            out_specs=[pl.BlockSpec(memory_space=pltpu.VMEM)] * 2,
            scratch_shapes=[pltpu.SemaphoreType.DMA((2,))],
        ),
        out_shape=[pltpu.VMEM(shape, tokens.dtype)] * 2,
        cost_estimate=cost(0, 2 * tokens.size),
        name="first_cuts",
    )(member.astype(jnp.int32).reshape(1), tokens)


def project_kernel(sets, weights_at, totals_at, update, plan_ref, *refs):
    out_ref = refs[-1]
    for number, terms in enumerate(sets):
        total = None
        for array, at, weight in terms:
            part = jnp.dot(
                view(refs[array], at), refs[weights_at + weight][...], preferred_element_type=jnp.float32
            )
            total = part if total is None else total + part
        if totals_at:
            before = refs[totals_at[number]][...]
            total = before if total is None else total + before
        if update is None:
            out_ref[number] = total
        else:
            shrink_at, panels_at = update
            shrink = refs[shrink_at][...]
            for block, panel in enumerate(panels_at):
                rank = refs[panel].shape[0]
                term = jnp.dot(
                    shrink[:, block * rank : (block + 1) * rank],
                    refs[panel][...],
                    preferred_element_type=jnp.float32,
                )
                span = slice(block * BLOCK, (block + 1) * BLOCK)
                out_ref[span, :] = (total[span] + adapter_scale * term).astype(out_ref.dtype)


def project(sets, weight, tile, plan, rows, total=None, update=None, into=None, weigh=2, name=None):
    columns = weight.shape[1]
    known, spans, flat = Arrays(), [], []
    for terms in sets:
        flat.append([])
        for array, at, k, span in terms:
            if (k, span) not in spans:
                spans.append((k, span))
            flat[-1].append((known.place(array), at, spans.index((k, span))))
    depth = weight.shape[0] // 4
    operands = list(known.arrays)
    in_specs = [whole_spec(a) for a in operands]
    weights_at = len(operands)
    for k, span in spans:
        if k is None:
            in_specs.append(pl.BlockSpec((depth, tile), lambda n, plan, span=span: (span, n)))
        else:
            in_specs.append(
                pl.BlockSpec((depth * span, tile), lambda n, plan, k=k, span=span: (plan[k] // span, n))
            )
        operands.append(weight)
    totals_at = []
    if total is not None:
        total = pltpu.with_memory_space_constraint(total, pltpu.HBM)
        for number in range(len(sets)):
            in_specs.append(pl.BlockSpec((None, rows, tile), lambda n, plan, number=number: (number, 0, n)))
            operands.append(total)
            totals_at.append(len(operands) - 1)
    updating, aliases = None, {}
    if update is None:
        out_shape = pltpu.HBM((len(sets), rows, columns), jnp.float32)
        out_spec = pl.BlockSpec((len(sets), rows, tile), lambda n, plan: (0, 0, n))
    else:
        first_set, shrink, panels = update
        panels = pltpu.with_memory_space_constraint(panels, pltpu.HBM)
        in_specs.append(whole_spec(shrink))
        operands.append(shrink)
        shrink_at, panels_at = len(operands) - 1, []
        for block in range(rows // BLOCK):
            index = PANELS_AT + first_set * (rows // BLOCK) + block
            in_specs.append(
                pl.BlockSpec((None, panels.shape[1], tile), lambda n, plan, index=index: (plan[index], 0, n))
            )
            operands.append(panels)
            panels_at.append(len(operands) - 1)
        updating = (shrink_at, panels_at)
        out_shape = jax.ShapeDtypeStruct(into.shape, into.dtype)
        out_spec = pl.BlockSpec((rows, tile), lambda n, plan: (plan[first_set], n))
        in_specs.append(pl.BlockSpec(memory_space=pl.ANY))
        operands.append(into)
        aliases = {len(operands): 0}
    products = sum(1 if k is None else span for terms in sets for _, _, k, span in terms)
    products *= rows * depth
    moved = 2 * products // rows * columns + 4 * len(sets) * rows * columns * (1 if total is None else 2)
    return pl.pallas_call(
        functools.partial(project_kernel, flat, weights_at, totals_at, updating),
        grid_spec=pltpu.PrefetchScalarGridSpec(
            num_scalar_prefetch=1,
            grid=(columns // tile,),
            in_specs=in_specs,
            out_specs=out_spec,
        ),
        out_shape=out_shape,
        input_output_aliases=aliases,
        cost_estimate=cost(int(weigh * 2 * products * columns), int(weigh * moved)),
        compiler_params=pltpu.CompilerParams(vmem_limit_bytes=VMEM_BYTES),
        name=name,
    )(plan, *operands)


def finish_kernel(count, plan_ref, *refs):
    own_ref, near_ref, panel_one, panel_two, out_ref = refs[0], refs[1], refs[-3], refs[-2], refs[-1]
    number = pl.program_id(0)
    shrink = refs[2][...]
    for other in range(1, count):
        shrink = jnp.where(number == other, refs[2 + other][...], shrink)
    rank = panel_one.shape[0]
    for block, panel in enumerate((panel_one, panel_two)):
        term = adapter_scale * jnp.dot(
            shrink[:, block * rank : (block + 1) * rank], panel[...], preferred_element_type=jnp.float32
        )
        span = slice(block * BLOCK, (block + 1) * BLOCK)

        @pl.when(number == 0)
        def _():
            out_ref[span, :] = (own_ref[span] + term).astype(out_ref.dtype)

        @pl.when(number != 0)
        def _():
            out_ref[span, :] = (near_ref[span] + term).astype(out_ref.dtype)


def finish(own, near, shrinks, panels, plan, row_total):
    _, rows, columns = near.shape
    rank = panels.shape[1]
    own, near, panels = (pltpu.with_memory_space_constraint(array, pltpu.HBM) for array in (own, near, panels))
    tile = tile_of(columns, 2560)
    return pl.pallas_call(
        functools.partial(finish_kernel, 3),
        grid_spec=pltpu.PrefetchScalarGridSpec(
            num_scalar_prefetch=1,
            grid=(3, columns // tile),
            in_specs=[
                pl.BlockSpec((None, rows, tile), lambda s, n, plan: (0, 0, jnp.where(s == 0, n, columns // tile - 1))),
                pl.BlockSpec((None, rows, tile), lambda s, n, plan: (jnp.maximum(s - 1, 0), 0, n)),
            ]
            + [whole_spec(shrink) for shrink in shrinks]
            + [
                pl.BlockSpec(
                    (None, rank, tile), lambda s, n, plan, block=block: (plan[PANELS_AT + 2 * s + block], 0, n)
                )
                for block in range(2)
            ],
            out_specs=pl.BlockSpec((rows, tile), lambda s, n, plan: (plan[s], n)),
        ),
        out_shape=jax.ShapeDtypeStruct((row_total, columns), jnp.bfloat16),
        cost_estimate=cost(12 * rows * rank * columns, 18 * rows * columns),
        compiler_params=pltpu.CompilerParams(vmem_limit_bytes=VMEM_BYTES),
        name="finish_rows",
    )(plan, own, near, *shrinks, panels, panels)


def shrink_kernel(sets, panels_at, plan_ref, *refs):
    panels_ref = refs[panels_at]
    rank = panels_ref.shape[1]
    nt = (((1,), (1,)), ((), ()))
    for number, (terms, out_ref) in enumerate(zip(sets, refs[panels_at + 1 :])):
        blocks = refs[terms[0][0]].shape[-2] // BLOCK
        for block in range(blocks):
            panel = plan_ref[PANELS_AT + number * blocks + block]
            total = 0
            for array, at, start in terms:
                tokens = view(refs[array], at)[block * BLOCK : (block + 1) * BLOCK]
                total += lax.dot_general(
                    tokens,
                    panels_ref[panel, :, start : start + tokens.shape[1]],
                    nt,
                    preferred_element_type=jnp.float32,
                )
            out_ref[:, block * rank : (block + 1) * rank] = total


def shrink_parts(tokens, sets, panels, plan):
    rows, width = tokens.shape
    known = Arrays()
    flat = [[(known.place(tokens), None, 0)]]
    flat += [[(known.place(array), at, start) for array, at, start in terms] for terms in sets]
    operands = known.arrays + [panels]
    _, rank, depth = panels.shape
    shape = (BLOCK, rank * (rows // BLOCK))
    in_specs = [whole_spec(a) for a in operands]
    in_specs[0] = pl.BlockSpec((rows, depth), lambda i, plan: (0, plan[0]))
    return pl.pallas_call(
        functools.partial(shrink_kernel, flat, len(known.arrays)),
        grid_spec=pltpu.PrefetchScalarGridSpec(
            num_scalar_prefetch=1,
            grid=(1,),
            in_specs=in_specs,
            out_specs=[pl.BlockSpec(shape, lambda *_: (0, 0))] * len(flat),
        ),
        out_shape=[jax.ShapeDtypeStruct(shape, jnp.float32)] * len(flat),
        cost_estimate=cost(8 * len(flat) * rows * depth * rank, 2 * (panels.size + len(flat) * rows * depth)),
        compiler_params=pltpu.CompilerParams(vmem_limit_bytes=VMEM_BYTES),
        name="shrink_parts",
    )(plan, *operands)


def after(value, *others):
    return lax.optimization_barrier((value,) + others)[0]


def square(tokens, frozen_weight, down_weight, up_weight, owners, select_slot):
    group = lax.axis_index("grp")
    member = lax.axis_index("tp")
    rows, width = tokens.shape
    blocks = rows // BLOCK
    depth = width // 4
    to_x = lambda v: lax.ppermute(v, "tp", [(i, i ^ 1) for i in range(4)])
    to_y = lambda v: lax.ppermute(v, "tp", [(i, i ^ 2) for i in range(4)])
    across = lambda v: lax.ppermute(v, "tp", [(i, i ^ 3) for i in range(4)])

    members = member ^ jnp.arange(4, dtype=jnp.int32)
    mine = lax.dynamic_slice_in_dim(owners, group * 4 * blocks, 4 * blocks).reshape(4, blocks)
    mine = jnp.sum(jnp.where((members[:, None] == jnp.arange(4))[:, :, None], mine[None], 0), axis=1)
    plan = jnp.concatenate([members, mine.reshape(-1)]).astype(jnp.int32)

    def part(array, start, size):
        return lax.dynamic_slice(array, (0, start), (rows, size))

    def cut(j, *others):
        return part(tokens, after((member ^ 3 ^ j) * depth, *others), depth)

    s0, s3 = first_cuts(tokens, member)
    x0, y3 = to_x(s0), to_y(s3)
    s1, s2 = cut(1, s0, s3), cut(2, s0, s3)
    x1, y2 = to_x(s1), to_y(s2)
    x2, y1 = to_x(after(s2, x0, y3)), to_y(after(s1, x0, y3))

    def chosen(panels, select):
        return jnp.take(panels, select, axis=0, mode="clip")

    def exchange(panels):
        return lax.all_to_all(panels, "grp", split_axis=0, concat_axis=0, tiled=True)

    down_out = chosen(down_weight, after(select_slot, s0, s3))
    down = exchange(down_out)

    own = project(
        [[(tokens, (i * depth, (i + 1) * depth), None, i) for i in range(4)]],
        frozen_weight, tile_of(frozen_weight.shape[1], 256), after(plan, down_out), rows, weigh=0, name="own_rows",
    )

    tile = tile_of(frozen_weight.shape[1], 512)

    d0, d3 = to_y(after(x0, x1, y2)), to_x(after(y3, x1, y2))
    near = project(
        [[(x0, None, 2, 1), (x1, None, 3, 1)], [(y3, None, 2, 1), (y2, None, 3, 1)]],
        frozen_weight, tile, after(plan, own), rows, weigh=6, name="near_rows",
    )
    up = exchange(chosen(up_weight, after(select_slot, down, near)))
    x3, y0 = to_x(after(s3, x2, y1)), to_y(after(s0, x2, y1))
    near = project(
        [[(x2, None, 0, 1)], [(y1, None, 0, 1)]],
        frozen_weight, tile, plan, rows, total=near, weigh=0, name="near_rows_more",
    )

    share = shrink_parts(tokens, [[(x2, None, 0)], [(y1, None, 0)], [(d0, None, 0)]], down, after(plan, near, d3))
    home = share[0] + to_x(share[1]) + to_y(share[2]) + across(share[3])
    home = home.astype(jnp.bfloat16)
    shrinks = [home, to_x(home), to_y(home), across(home)]
    d1, d2 = to_y(after(x1, home)), to_x(after(y2, home))

    far = project(
        [[(d0, None, 0, 1), (d3, None, 3, 1)]],
        frozen_weight, tile_of(frozen_weight.shape[1], 640), after(plan, share[0]), rows, weigh=4, name="far_rows",
    )
    near = project(
        [[(x3, None, 1, 1)], [(y0, None, 1, 1)]],
        frozen_weight, tile, after(plan, home, far), rows, total=near, weigh=4, name="near_rows_rest",
    )
    out = finish(own, near, shrinks[:3], up, plan, 4 * rows)
    return project(
        [[(d1, None, 1, 1), (d2, None, 2, 1)]],
        frozen_weight, tile_of(frozen_weight.shape[1], 640), plan, rows,
        total=far, update=(3, shrinks[3], up), into=out, name="last_rows",
    )


def general(tokens, frozen_weight, down_weight, up_weight, owners, select_slot):
    tp_count = lax.axis_size("tp")
    group = lax.axis_index("grp")
    member = lax.axis_index("tp")
    local_rows, width = tokens.shape
    group_rows = local_rows * tp_count
    blocks_here = group_rows // BLOCK
    rank_columns = down_weight.shape[1]
    column_slice = up_weight.shape[2]
    my_owners = lax.dynamic_slice_in_dim(owners, group * blocks_here, blocks_here)
    arrived_a, arrived_b = (
        lax.all_to_all(
            jnp.take(panels, select_slot, axis=0), "grp", split_axis=0, concat_axis=0, tiled=True
        )
        for panels in (down_weight, up_weight)
    )
    down_tile = jnp.take(arrived_a, my_owners, axis=0)
    up_tile = jnp.take(arrived_b, my_owners, axis=0)
    whole_a = lax.all_gather(down_tile, "tp", axis=2, tiled=True)
    span_rows = min(local_rows, BLOCK)
    pieces_here = local_rows // span_rows
    first_block = member * local_rows // BLOCK
    local_a = lax.dynamic_slice_in_dim(whole_a, first_block, pieces_here, 0)
    shrink_local = jnp.einsum(
        "pnd,prd->pnr",
        tokens.reshape(pieces_here, span_rows, width),
        local_a,
        preferred_element_type=jnp.float32,
    )
    shrink_local = shrink_local.astype(jnp.bfloat16).reshape(local_rows, rank_columns)
    shrink = lax.all_gather(shrink_local, "tp", axis=0, tiled=True)
    frozen_rows = jnp.dot(
        lax.all_gather(tokens, "tp", axis=0, tiled=True),
        frozen_weight,
        preferred_element_type=jnp.float32,
    )
    update_rows = jnp.einsum(
        "bnr,brc->bnc",
        shrink.reshape(blocks_here, BLOCK, rank_columns),
        up_tile,
        preferred_element_type=jnp.float32,
    )
    update_rows = update_rows.reshape(group_rows, column_slice)
    return (frozen_rows + adapter_scale * update_rows).astype(jnp.bfloat16)


def local(tokens, frozen_weight, down_weight, up_weight, adapter_storage_slot, adapter_of_block):
    group_count = lax.axis_size("grp")
    group = lax.axis_index("grp")
    loaded_here = down_weight.shape[0]
    adapters = jnp.arange(adapter_storage_slot.shape[0])
    named = adapter_of_block[:, None] == adapters[None, :]
    slot_numbers = jnp.sum(jnp.where(named, adapter_storage_slot[None, :], 0), axis=1)
    owners = slot_numbers // loaded_here
    offsets = slot_numbers % loaded_here
    owned_here = owners.reshape(group_count, -1) == group
    select_slot = jnp.sum(jnp.where(owned_here, offsets.reshape(group_count, -1), 0), axis=1)
    fits = lax.axis_size("tp") == 4 and tokens.shape[0] == 2 * BLOCK
    way = square if fits else general
    return way(tokens, frozen_weight, down_weight, up_weight, owners, select_slot)


def solution(mesh):
    placed = (
        P(("grp", "tp"), None),
        P(None, "tp"),
        P("grp", None, "tp"),
        P("grp", None, "tp"),
        P(),
        P(),
    )
    return jax.shard_map(
        local, mesh=mesh, in_specs=placed, out_specs=P("grp", "tp"), check_vma=False
    )
```

```python
import functools

import jax
import jax.numpy as jnp
from jax import lax
from jax.experimental import pallas as pl
from jax.experimental.pallas import tpu as pltpu
from jax.sharding import PartitionSpec as P

BLOCK = 128
MIB = 1 << 20
PANELS_AT = 4
VMEM_BYTES = 24 * MIB

adapter_scale = 0.5


def tile_of(columns, most):
    return max(t for t in range(128, most + 1, 128) if columns % t == 0)


def whole_spec(array):
    zeros = (0,) * array.ndim
    return pl.BlockSpec(array.shape, lambda *_: zeros)


def cost(flops, moved):
    return pl.CostEstimate(flops=flops, bytes_accessed=moved, transcendentals=0)


class Arrays:
    def __init__(self):
        self.arrays = []

    def place(self, array):
        for number, known in enumerate(self.arrays):
            if known is array:
                return number
        self.arrays.append(array)
        return len(self.arrays) - 1


def view(ref, at):
    return ref[...] if at is None else ref[:, at[0] : at[1]]


def cut_kernel(flips, member_ref, tokens_ref, one_ref, two_ref, sems):
    depth = one_ref.shape[1]
    copies = []
    for number, (out_ref, flip) in enumerate(zip((one_ref, two_ref), flips)):
        start = pl.multiple_of((member_ref[0] ^ flip) * depth, depth)
        copies.append(pltpu.make_async_copy(tokens_ref.at[:, pl.ds(start, depth)], out_ref, sems.at[number]))
    for copy in copies:
        copy.start()
    for copy in copies:
        copy.wait()


def cuts(tokens, member, flips):
    rows, width = tokens.shape
    shape = (rows, width // 4)
    return pl.pallas_call(
        functools.partial(cut_kernel, flips),
        grid_spec=pltpu.PrefetchScalarGridSpec(
            num_scalar_prefetch=1,
            grid=(1,),
            in_specs=[pl.BlockSpec(memory_space=pl.ANY)],
            out_specs=[pl.BlockSpec(memory_space=pltpu.VMEM)] * 2,
            scratch_shapes=[pltpu.SemaphoreType.DMA((2,))],
        ),
        out_shape=[pltpu.VMEM(shape, tokens.dtype)] * 2,
        cost_estimate=cost(0, 2 * tokens.size),
        name="cuts",
    )(member.astype(jnp.int32).reshape(1), tokens)


def project_kernel(sets, weights_at, totals_at, update, plan_ref, *refs):
    out_ref = refs[-1]
    for number, terms in enumerate(sets):
        total = None
        for array, at, weight in terms:
            part = jnp.dot(
                view(refs[array], at), refs[weights_at + weight][...], preferred_element_type=jnp.float32
            )
            total = part if total is None else total + part
        if totals_at:
            before = refs[totals_at[number]][...]
            total = before if total is None else total + before
        if update is None:
            out_ref[number] = total
        else:
            shrink_at, panels_at = update
            shrink = refs[shrink_at][...]
            for block, panel in enumerate(panels_at):
                rank = refs[panel].shape[0]
                term = jnp.dot(
                    shrink[:, block * rank : (block + 1) * rank],
                    refs[panel][...],
                    preferred_element_type=jnp.float32,
                )
                span = slice(block * BLOCK, (block + 1) * BLOCK)
                out_ref[span, :] = (total[span] + adapter_scale * term).astype(out_ref.dtype)


def project(sets, weight, tile, plan, rows, total=None, update=None, into=None, weigh=2, name=None):
    columns = weight.shape[1]
    known, spans, flat = Arrays(), [], []
    for terms in sets:
        flat.append([])
        for array, at, k, span in terms:
            if (k, span) not in spans:
                spans.append((k, span))
            flat[-1].append((known.place(array), at, spans.index((k, span))))
    depth = weight.shape[0] // 4
    operands = list(known.arrays)
    in_specs = [whole_spec(a) for a in operands]
    weights_at = len(operands)
    for k, span in spans:
        if k is None:
            in_specs.append(pl.BlockSpec((depth, tile), lambda n, plan, span=span: (span, n)))
        else:
            in_specs.append(
                pl.BlockSpec((depth * span, tile), lambda n, plan, k=k, span=span: (plan[k] // span, n))
            )
        operands.append(weight)
    totals_at = []
    if total is not None:
        total = pltpu.with_memory_space_constraint(total, pltpu.HBM)
        for number in range(len(sets)):
            in_specs.append(pl.BlockSpec((None, rows, tile), lambda n, plan, number=number: (number, 0, n)))
            operands.append(total)
            totals_at.append(len(operands) - 1)
    updating, aliases = None, {}
    if update is None:
        out_shape = pltpu.HBM((len(sets), rows, columns), jnp.float32)
        out_spec = pl.BlockSpec((len(sets), rows, tile), lambda n, plan: (0, 0, n))
    else:
        first_set, shrink, panels = update
        panels = pltpu.with_memory_space_constraint(panels, pltpu.HBM)
        in_specs.append(whole_spec(shrink))
        operands.append(shrink)
        shrink_at, panels_at = len(operands) - 1, []
        for block in range(rows // BLOCK):
            index = PANELS_AT + first_set * (rows // BLOCK) + block
            in_specs.append(
                pl.BlockSpec((None, panels.shape[1], tile), lambda n, plan, index=index: (plan[index], 0, n))
            )
            operands.append(panels)
            panels_at.append(len(operands) - 1)
        updating = (shrink_at, panels_at)
        out_shape = jax.ShapeDtypeStruct(into.shape, into.dtype)
        out_spec = pl.BlockSpec((rows, tile), lambda n, plan: (plan[first_set], n))
        in_specs.append(pl.BlockSpec(memory_space=pl.ANY))
        operands.append(into)
        aliases = {len(operands): 0}
    products = sum(1 if k is None else span for terms in sets for _, _, k, span in terms)
    products *= rows * depth
    moved = 2 * products // rows * columns + 4 * len(sets) * rows * columns * (1 if total is None else 2)
    return pl.pallas_call(
        functools.partial(project_kernel, flat, weights_at, totals_at, updating),
        grid_spec=pltpu.PrefetchScalarGridSpec(
            num_scalar_prefetch=1,
            grid=(columns // tile,),
            in_specs=in_specs,
            out_specs=out_spec,
        ),
        out_shape=out_shape,
        input_output_aliases=aliases,
        cost_estimate=cost(int(weigh * 2 * products * columns), int(weigh * moved)),
        compiler_params=pltpu.CompilerParams(vmem_limit_bytes=VMEM_BYTES),
        name=name,
    )(plan, *operands)


def finish_kernel(count, plan_ref, *refs):
    own_ref, near_ref, panel_one, panel_two, out_ref = refs[0], refs[1], refs[-3], refs[-2], refs[-1]
    number = pl.program_id(0)
    shrink = refs[2][...]
    for other in range(1, count):
        shrink = jnp.where(number == other, refs[2 + other][...], shrink)
    rank = panel_one.shape[0]
    for block, panel in enumerate((panel_one, panel_two)):
        term = adapter_scale * jnp.dot(
            shrink[:, block * rank : (block + 1) * rank], panel[...], preferred_element_type=jnp.float32
        )
        span = slice(block * BLOCK, (block + 1) * BLOCK)

        @pl.when(number == 0)
        def _():
            out_ref[span, :] = (own_ref[span] + term).astype(out_ref.dtype)

        @pl.when(number != 0)
        def _():
            out_ref[span, :] = (near_ref[span] + term).astype(out_ref.dtype)


def finish(own, near, shrinks, panels, plan, row_total):
    _, rows, columns = near.shape
    rank = panels.shape[1]
    own, near, panels = (pltpu.with_memory_space_constraint(array, pltpu.HBM) for array in (own, near, panels))
    tile = tile_of(columns, 2560)
    return pl.pallas_call(
        functools.partial(finish_kernel, 3),
        grid_spec=pltpu.PrefetchScalarGridSpec(
            num_scalar_prefetch=1,
            grid=(3, columns // tile),
            in_specs=[
                pl.BlockSpec((None, rows, tile), lambda s, n, plan: (0, 0, jnp.where(s == 0, n, columns // tile - 1))),
                pl.BlockSpec((None, rows, tile), lambda s, n, plan: (jnp.maximum(s - 1, 0), 0, n)),
            ]
            + [whole_spec(shrink) for shrink in shrinks]
            + [
                pl.BlockSpec(
                    (None, rank, tile), lambda s, n, plan, block=block: (plan[PANELS_AT + 2 * s + block], 0, n)
                )
                for block in range(2)
            ],
            out_specs=pl.BlockSpec((rows, tile), lambda s, n, plan: (plan[s], n)),
        ),
        out_shape=jax.ShapeDtypeStruct((row_total, columns), jnp.bfloat16),
        cost_estimate=cost(12 * rows * rank * columns, 18 * rows * columns),
        compiler_params=pltpu.CompilerParams(vmem_limit_bytes=VMEM_BYTES),
        name="finish_rows",
    )(plan, own, near, *shrinks, panels, panels)


def shrink_kernel(sets, panels_at, plan_ref, *refs):
    panels_ref = refs[panels_at]
    rank = panels_ref.shape[1]
    nt = (((1,), (1,)), ((), ()))
    for number, (terms, out_ref) in enumerate(zip(sets, refs[panels_at + 1 :])):
        blocks = refs[terms[0][0]].shape[-2] // BLOCK
        for block in range(blocks):
            panel = plan_ref[PANELS_AT + number * blocks + block]
            total = 0
            for array, at, start in terms:
                tokens = view(refs[array], at)[block * BLOCK : (block + 1) * BLOCK]
                total += lax.dot_general(
                    tokens,
                    panels_ref[panel, :, start : start + tokens.shape[1]],
                    nt,
                    preferred_element_type=jnp.float32,
                )
            out_ref[:, block * rank : (block + 1) * rank] = total


def shrink_parts(tokens, sets, panels, plan):
    rows, width = tokens.shape
    known = Arrays()
    flat = [[(known.place(tokens), None, 0)]]
    flat += [[(known.place(array), at, start) for array, at, start in terms] for terms in sets]
    operands = known.arrays + [panels]
    _, rank, depth = panels.shape
    shape = (BLOCK, rank * (rows // BLOCK))
    in_specs = [whole_spec(a) for a in operands]
    in_specs[0] = pl.BlockSpec((rows, depth), lambda i, plan: (0, plan[0]))
    return pl.pallas_call(
        functools.partial(shrink_kernel, flat, len(known.arrays)),
        grid_spec=pltpu.PrefetchScalarGridSpec(
            num_scalar_prefetch=1,
            grid=(1,),
            in_specs=in_specs,
            out_specs=[pl.BlockSpec(shape, lambda *_: (0, 0))] * len(flat),
        ),
        out_shape=[jax.ShapeDtypeStruct(shape, jnp.float32)] * len(flat),
        cost_estimate=cost(8 * len(flat) * rows * depth * rank, 2 * (panels.size + len(flat) * rows * depth)),
        compiler_params=pltpu.CompilerParams(vmem_limit_bytes=VMEM_BYTES),
        name="shrink_parts",
    )(plan, *operands)


def after(value, *others):
    return lax.optimization_barrier((value,) + others)[0]


def square(tokens, frozen_weight, down_weight, up_weight, owners, select_slot):
    group = lax.axis_index("grp")
    member = lax.axis_index("tp")
    rows, width = tokens.shape
    blocks = rows // BLOCK
    depth = width // 4
    to_x = lambda v: lax.ppermute(v, "tp", [(i, i ^ 1) for i in range(4)])
    to_y = lambda v: lax.ppermute(v, "tp", [(i, i ^ 2) for i in range(4)])
    across = lambda v: lax.ppermute(v, "tp", [(i, i ^ 3) for i in range(4)])

    members = member ^ jnp.arange(4, dtype=jnp.int32)
    mine = lax.dynamic_slice_in_dim(owners, group * 4 * blocks, 4 * blocks).reshape(4, blocks)
    mine = jnp.sum(jnp.where((members[:, None] == jnp.arange(4))[:, :, None], mine[None], 0), axis=1)
    plan = jnp.concatenate([members, mine.reshape(-1)]).astype(jnp.int32)

    s0, s3 = cuts(tokens, member, (3, 0))
    x0, y3 = to_x(s0), to_y(s3)
    s1, s2 = cuts(tokens, after(member, s0, s3), (2, 1))
    x1, y2 = to_x(s1), to_y(s2)
    x2, y1 = to_x(after(s2, x0, y3)), to_y(after(s1, x0, y3))

    def chosen(panels, select):
        return jnp.take(panels, select, axis=0, mode="clip")

    def exchange(panels):
        return lax.all_to_all(panels, "grp", split_axis=0, concat_axis=0, tiled=True)

    down_out = chosen(down_weight, after(select_slot, s0, s3))
    down = exchange(down_out)

    own = project(
        [[(tokens, (i * depth, (i + 1) * depth), None, i) for i in range(4)]],
        frozen_weight, tile_of(frozen_weight.shape[1], 256), after(plan, down_out), rows, weigh=0, name="own_rows",
    )

    tile = tile_of(frozen_weight.shape[1], 512)

    d0, d3 = to_y(after(x0, x1, y2)), to_x(after(y3, x1, y2))
    near = project(
        [[(x0, None, 2, 1), (x1, None, 3, 1)], [(y3, None, 2, 1), (y2, None, 3, 1)]],
        frozen_weight, tile, after(plan, own), rows, weigh=6, name="near_rows",
    )
    up = exchange(chosen(up_weight, after(select_slot, down, near)))
    x3, y0 = to_x(after(s3, x2, y1)), to_y(after(s0, x2, y1))
    near = project(
        [[(x2, None, 0, 1)], [(y1, None, 0, 1)]],
        frozen_weight, tile, plan, rows, total=near, weigh=0, name="near_rows_more",
    )

    share = shrink_parts(tokens, [[(x2, None, 0)], [(y1, None, 0)], [(d0, None, 0)]], down, after(plan, near, d3))
    home = share[0] + to_x(share[1]) + to_y(share[2]) + across(share[3])
    home = home.astype(jnp.bfloat16)
    shrinks = [home, to_x(home), to_y(home), across(home)]
    d1, d2 = to_y(after(x1, home)), to_x(after(y2, home))

    far = project(
        [[(d0, None, 0, 1), (d3, None, 3, 1)]],
        frozen_weight, tile_of(frozen_weight.shape[1], 640), after(plan, share[0]), rows, weigh=4, name="far_rows",
    )
    near = project(
        [[(x3, None, 1, 1)], [(y0, None, 1, 1)]],
        frozen_weight, tile, after(plan, home, far), rows, total=near, weigh=4, name="near_rows_rest",
    )
    out = finish(own, near, shrinks[:3], up, plan, 4 * rows)
    return project(
        [[(d1, None, 1, 1), (d2, None, 2, 1)]],
        frozen_weight, tile_of(frozen_weight.shape[1], 640), plan, rows,
        total=far, update=(3, shrinks[3], up), into=out, name="last_rows",
    )


def general(tokens, frozen_weight, down_weight, up_weight, owners, select_slot):
    tp_count = lax.axis_size("tp")
    group = lax.axis_index("grp")
    member = lax.axis_index("tp")
    local_rows, width = tokens.shape
    group_rows = local_rows * tp_count
    blocks_here = group_rows // BLOCK
    rank_columns = down_weight.shape[1]
    column_slice = up_weight.shape[2]
    my_owners = lax.dynamic_slice_in_dim(owners, group * blocks_here, blocks_here)
    arrived_a, arrived_b = (
        lax.all_to_all(
            jnp.take(panels, select_slot, axis=0), "grp", split_axis=0, concat_axis=0, tiled=True
        )
        for panels in (down_weight, up_weight)
    )
    down_tile = jnp.take(arrived_a, my_owners, axis=0)
    up_tile = jnp.take(arrived_b, my_owners, axis=0)
    whole_a = lax.all_gather(down_tile, "tp", axis=2, tiled=True)
    span_rows = min(local_rows, BLOCK)
    pieces_here = local_rows // span_rows
    first_block = member * local_rows // BLOCK
    local_a = lax.dynamic_slice_in_dim(whole_a, first_block, pieces_here, 0)
    shrink_local = jnp.einsum(
        "pnd,prd->pnr",
        tokens.reshape(pieces_here, span_rows, width),
        local_a,
        preferred_element_type=jnp.float32,
    )
    shrink_local = shrink_local.astype(jnp.bfloat16).reshape(local_rows, rank_columns)
    shrink = lax.all_gather(shrink_local, "tp", axis=0, tiled=True)
    frozen_rows = jnp.dot(
        lax.all_gather(tokens, "tp", axis=0, tiled=True),
        frozen_weight,
        preferred_element_type=jnp.float32,
    )
    update_rows = jnp.einsum(
        "bnr,brc->bnc",
        shrink.reshape(blocks_here, BLOCK, rank_columns),
        up_tile,
        preferred_element_type=jnp.float32,
    )
    update_rows = update_rows.reshape(group_rows, column_slice)
    return (frozen_rows + adapter_scale * update_rows).astype(jnp.bfloat16)


def local(tokens, frozen_weight, down_weight, up_weight, adapter_storage_slot, adapter_of_block):
    group_count = lax.axis_size("grp")
    group = lax.axis_index("grp")
    loaded_here = down_weight.shape[0]
    adapters = jnp.arange(adapter_storage_slot.shape[0])
    named = adapter_of_block[:, None] == adapters[None, :]
    slot_numbers = jnp.sum(jnp.where(named, adapter_storage_slot[None, :], 0), axis=1)
    owners = slot_numbers // loaded_here
    offsets = slot_numbers % loaded_here
    owned_here = owners.reshape(group_count, -1) == group
    select_slot = jnp.sum(jnp.where(owned_here, offsets.reshape(group_count, -1), 0), axis=1)
    fits = lax.axis_size("tp") == 4 and tokens.shape[0] == 2 * BLOCK
    way = square if fits else general
    return way(tokens, frozen_weight, down_weight, up_weight, owners, select_slot)


def solution(mesh):
    placed = (
        P(("grp", "tp"), None),
        P(None, "tp"),
        P("grp", None, "tp"),
        P("grp", None, "tp"),
        P(),
        P(),
    )
    return jax.shard_map(
        local, mesh=mesh, in_specs=placed, out_specs=P("grp", "tp"), check_vma=False
    )
```

```python
import functools

import jax
import jax.numpy as jnp
from jax import lax
from jax.experimental import pallas as pl
from jax.experimental.pallas import tpu as pltpu
from jax.sharding import PartitionSpec as P

BLOCK = 128
MIB = 1 << 20
PANELS_AT = 4
VMEM_BYTES = 36 * MIB

adapter_scale = 0.5


def tile_of(columns, most):
    return max(t for t in range(128, most + 1, 128) if columns % t == 0)


def whole_spec(array):
    zeros = (0,) * array.ndim
    return pl.BlockSpec(array.shape, lambda *_: zeros)


def cost(flops, moved):
    return pl.CostEstimate(flops=flops, bytes_accessed=moved, transcendentals=0)


class Arrays:
    def __init__(self):
        self.arrays = []

    def place(self, array):
        for number, known in enumerate(self.arrays):
            if known is array:
                return number
        self.arrays.append(array)
        return len(self.arrays) - 1


def view(ref, at):
    return ref[...] if at is None else ref[:, at[0] : at[1]]


def cut_kernel(member_ref, tokens_ref, far_ref, own_ref, sems):
    depth = far_ref.shape[1]
    copies = []
    for number, (out_ref, flip) in enumerate(((far_ref, 3), (own_ref, 0))):
        start = pl.multiple_of((member_ref[0] ^ flip) * depth, depth)
        copies.append(pltpu.make_async_copy(tokens_ref.at[:, pl.ds(start, depth)], out_ref, sems.at[number]))
    for copy in copies:
        copy.start()
    for copy in copies:
        copy.wait()


def first_cuts(tokens, member):
    rows, width = tokens.shape
    shape = (rows, width // 4)
    return pl.pallas_call(
        cut_kernel,
        grid_spec=pltpu.PrefetchScalarGridSpec(
            num_scalar_prefetch=1,
            grid=(1,),
            in_specs=[pl.BlockSpec(memory_space=pl.ANY)],
            out_specs=[pl.BlockSpec(memory_space=pltpu.VMEM)] * 2,
            scratch_shapes=[pltpu.SemaphoreType.DMA((2,))],
        ),
        out_shape=[pltpu.VMEM(shape, tokens.dtype)] * 2,
        cost_estimate=cost(0, 2 * tokens.size),
        name="first_cuts",
    )(member.astype(jnp.int32).reshape(1), tokens)


def project_kernel(sets, weights_at, totals_at, update, plan_ref, *refs):
    out_ref = refs[-1]
    for number, terms in enumerate(sets):
        total = None
        for array, at, weight in terms:
            part = jnp.dot(
                view(refs[array], at), refs[weights_at + weight][...], preferred_element_type=jnp.float32
            )
            total = part if total is None else total + part
        if totals_at:
            before = refs[totals_at[number]][...]
            total = before if total is None else total + before
        if update is None:
            out_ref[number] = total
        else:
            shrink_at, panels_at = update
            shrink = refs[shrink_at][...]
            for block, panel in enumerate(panels_at):
                rank = refs[panel].shape[0]
                term = jnp.dot(
                    shrink[:, block * rank : (block + 1) * rank],
                    refs[panel][...],
                    preferred_element_type=jnp.float32,
                )
                span = slice(block * BLOCK, (block + 1) * BLOCK)
                out_ref[span, :] = (total[span] + adapter_scale * term).astype(out_ref.dtype)


def project(sets, weight, tile, plan, rows, total=None, update=None, into=None, weigh=2, name=None):
    columns = weight.shape[1]
    known, spans, flat = Arrays(), [], []
    for terms in sets:
        flat.append([])
        for array, at, k, span in terms:
            if (k, span) not in spans:
                spans.append((k, span))
            flat[-1].append((known.place(array), at, spans.index((k, span))))
    depth = weight.shape[0] // 4
    operands = list(known.arrays)
    in_specs = [whole_spec(a) for a in operands]
    weights_at = len(operands)
    for k, span in spans:
        if k is None:
            in_specs.append(pl.BlockSpec((depth, tile), lambda n, plan, span=span: (span, n)))
        else:
            in_specs.append(
                pl.BlockSpec((depth * span, tile), lambda n, plan, k=k, span=span: (plan[k] // span, n))
            )
        operands.append(weight)
    totals_at = []
    if total is not None:
        total = pltpu.with_memory_space_constraint(total, pltpu.HBM)
        for number in range(len(sets)):
            in_specs.append(pl.BlockSpec((None, rows, tile), lambda n, plan, number=number: (number, 0, n)))
            operands.append(total)
            totals_at.append(len(operands) - 1)
    updating, aliases = None, {}
    if update is None:
        out_shape = pltpu.HBM((len(sets), rows, columns), jnp.float32)
        out_spec = pl.BlockSpec((len(sets), rows, tile), lambda n, plan: (0, 0, n))
    else:
        first_set, shrink, panels = update
        panels = pltpu.with_memory_space_constraint(panels, pltpu.HBM)
        in_specs.append(whole_spec(shrink))
        operands.append(shrink)
        shrink_at, panels_at = len(operands) - 1, []
        for block in range(rows // BLOCK):
            index = PANELS_AT + first_set * (rows // BLOCK) + block
            in_specs.append(
                pl.BlockSpec((None, panels.shape[1], tile), lambda n, plan, index=index: (plan[index], 0, n))
            )
            operands.append(panels)
            panels_at.append(len(operands) - 1)
        updating = (shrink_at, panels_at)
        out_shape = jax.ShapeDtypeStruct(into.shape, into.dtype)
        out_spec = pl.BlockSpec((rows, tile), lambda n, plan: (plan[first_set], n))
        in_specs.append(pl.BlockSpec(memory_space=pl.ANY))
        operands.append(into)
        aliases = {len(operands): 0}
    products = sum(1 if k is None else span for terms in sets for _, _, k, span in terms)
    products *= rows * depth
    moved = 2 * products // rows * columns + 4 * len(sets) * rows * columns * (1 if total is None else 2)
    return pl.pallas_call(
        functools.partial(project_kernel, flat, weights_at, totals_at, updating),
        grid_spec=pltpu.PrefetchScalarGridSpec(
            num_scalar_prefetch=1,
            grid=(columns // tile,),
            in_specs=in_specs,
            out_specs=out_spec,
        ),
        out_shape=out_shape,
        input_output_aliases=aliases,
        cost_estimate=cost(int(weigh * 2 * products * columns), int(weigh * moved)),
        compiler_params=pltpu.CompilerParams(vmem_limit_bytes=VMEM_BYTES),
        name=name,
    )(plan, *operands)


def finish_kernel(count, plan_ref, *refs):
    own_ref, near_ref, panel_one, panel_two, out_ref = refs[0], refs[1], refs[-3], refs[-2], refs[-1]
    number = pl.program_id(0)
    shrink = refs[2][...]
    for other in range(1, count):
        shrink = jnp.where(number == other, refs[2 + other][...], shrink)
    rank = panel_one.shape[0]
    for block, panel in enumerate((panel_one, panel_two)):
        term = adapter_scale * jnp.dot(
            shrink[:, block * rank : (block + 1) * rank], panel[...], preferred_element_type=jnp.float32
        )
        span = slice(block * BLOCK, (block + 1) * BLOCK)

        @pl.when(number == 0)
        def _():
            out_ref[span, :] = (own_ref[span] + term).astype(out_ref.dtype)

        @pl.when(number != 0)
        def _():
            out_ref[span, :] = (near_ref[span] + term).astype(out_ref.dtype)


def finish(own, near, shrinks, panels, plan, row_total):
    _, rows, columns = near.shape
    rank = panels.shape[1]
    own, near, panels = (pltpu.with_memory_space_constraint(array, pltpu.HBM) for array in (own, near, panels))
    tile = tile_of(columns, 2560)
    return pl.pallas_call(
        functools.partial(finish_kernel, 3),
        grid_spec=pltpu.PrefetchScalarGridSpec(
            num_scalar_prefetch=1,
            grid=(3, columns // tile),
            in_specs=[
                pl.BlockSpec((None, rows, tile), lambda s, n, plan: (0, 0, jnp.where(s == 0, n, columns // tile - 1))),
                pl.BlockSpec((None, rows, tile), lambda s, n, plan: (jnp.maximum(s - 1, 0), 0, n)),
            ]
            + [whole_spec(shrink) for shrink in shrinks]
            + [
                pl.BlockSpec(
                    (None, rank, tile), lambda s, n, plan, block=block: (plan[PANELS_AT + 2 * s + block], 0, n)
                )
                for block in range(2)
            ],
            out_specs=pl.BlockSpec((rows, tile), lambda s, n, plan: (plan[s], n)),
        ),
        out_shape=jax.ShapeDtypeStruct((row_total, columns), jnp.bfloat16),
        cost_estimate=cost(12 * rows * rank * columns, 18 * rows * columns),
        compiler_params=pltpu.CompilerParams(vmem_limit_bytes=VMEM_BYTES),
        name="finish_rows",
    )(plan, own, near, *shrinks, panels, panels)


def shrink_kernel(sets, panels_at, plan_ref, *refs):
    panels_ref = refs[panels_at]
    rank = panels_ref.shape[1]
    nt = (((1,), (1,)), ((), ()))
    for number, (terms, out_ref) in enumerate(zip(sets, refs[panels_at + 1 :])):
        blocks = refs[terms[0][0]].shape[-2] // BLOCK
        for block in range(blocks):
            panel = plan_ref[PANELS_AT + number * blocks + block]
            total = 0
            for array, at, start in terms:
                tokens = view(refs[array], at)[block * BLOCK : (block + 1) * BLOCK]
                total += lax.dot_general(
                    tokens,
                    panels_ref[panel, :, start : start + tokens.shape[1]],
                    nt,
                    preferred_element_type=jnp.float32,
                )
            out_ref[:, block * rank : (block + 1) * rank] = total


def shrink_parts(tokens, sets, panels, plan):
    rows, width = tokens.shape
    known = Arrays()
    flat = [[(known.place(tokens), None, 0)]]
    flat += [[(known.place(array), at, start) for array, at, start in terms] for terms in sets]
    operands = known.arrays + [panels]
    _, rank, depth = panels.shape
    shape = (BLOCK, rank * (rows // BLOCK))
    in_specs = [whole_spec(a) for a in operands]
    in_specs[0] = pl.BlockSpec((rows, depth), lambda i, plan: (0, plan[0]))
    return pl.pallas_call(
        functools.partial(shrink_kernel, flat, len(known.arrays)),
        grid_spec=pltpu.PrefetchScalarGridSpec(
            num_scalar_prefetch=1,
            grid=(1,),
            in_specs=in_specs,
            out_specs=[pl.BlockSpec(shape, lambda *_: (0, 0))] * len(flat),
        ),
        out_shape=[jax.ShapeDtypeStruct(shape, jnp.float32)] * len(flat),
        cost_estimate=cost(8 * len(flat) * rows * depth * rank, 2 * (panels.size + len(flat) * rows * depth)),
        compiler_params=pltpu.CompilerParams(vmem_limit_bytes=VMEM_BYTES),
        name="shrink_parts",
    )(plan, *operands)


def after(value, *others):
    return lax.optimization_barrier((value,) + others)[0]


def square(tokens, frozen_weight, down_weight, up_weight, owners, select_slot):
    group = lax.axis_index("grp")
    member = lax.axis_index("tp")
    rows, width = tokens.shape
    blocks = rows // BLOCK
    depth = width // 4
    to_x = lambda v: lax.ppermute(v, "tp", [(i, i ^ 1) for i in range(4)])
    to_y = lambda v: lax.ppermute(v, "tp", [(i, i ^ 2) for i in range(4)])
    across = lambda v: lax.ppermute(v, "tp", [(i, i ^ 3) for i in range(4)])

    members = member ^ jnp.arange(4, dtype=jnp.int32)
    mine = lax.dynamic_slice_in_dim(owners, group * 4 * blocks, 4 * blocks).reshape(4, blocks)
    mine = jnp.sum(jnp.where((members[:, None] == jnp.arange(4))[:, :, None], mine[None], 0), axis=1)
    plan = jnp.concatenate([members, mine.reshape(-1)]).astype(jnp.int32)

    def part(array, start, size):
        return lax.dynamic_slice(array, (0, start), (rows, size))

    def cut(j, *others):
        return part(tokens, after((member ^ 3 ^ j) * depth, *others), depth)

    s0, s3 = first_cuts(tokens, member)
    x0, y3 = to_x(s0), to_y(s3)
    s1, s2 = cut(1, s0, s3), cut(2, s0, s3)
    x1, y2 = to_x(s1), to_y(s2)
    x2, y1 = to_x(after(s2, x0, y3)), to_y(after(s1, x0, y3))

    def chosen(panels, select):
        return jnp.take(panels, select, axis=0, mode="clip")

    def exchange(panels):
        return lax.all_to_all(panels, "grp", split_axis=0, concat_axis=0, tiled=True)

    down_out = chosen(down_weight, after(select_slot, s0, s3))
    down = exchange(down_out)

    own = project(
        [[(tokens, (i * depth, (i + 1) * depth), None, i) for i in range(4)]],
        frozen_weight, tile_of(frozen_weight.shape[1], 256), after(plan, down_out), rows, weigh=0, name="own_rows",
    )

    tile = tile_of(frozen_weight.shape[1], 512)

    d0, d3 = to_y(after(x0, x1, y2)), to_x(after(y3, x1, y2))
    near = project(
        [[(x0, None, 2, 1), (x1, None, 3, 1)], [(y3, None, 2, 1), (y2, None, 3, 1)]],
        frozen_weight, tile, after(plan, own), rows, weigh=6, name="near_rows",
    )
    up = exchange(chosen(up_weight, after(select_slot, down, near)))
    x3, y0 = to_x(after(s3, x2, y1)), to_y(after(s0, x2, y1))
    near = project(
        [[(x2, None, 0, 1)], [(y1, None, 0, 1)]],
        frozen_weight, tile, plan, rows, total=near, weigh=0, name="near_rows_more",
    )

    share = shrink_parts(tokens, [[(x2, None, 0)], [(y1, None, 0)], [(d0, None, 0)]], down, after(plan, near, d3))
    home = share[0] + to_x(share[1]) + to_y(share[2]) + across(share[3])
    home = home.astype(jnp.bfloat16)
    shrinks = [home, to_x(home), to_y(home), across(home)]
    d1, d2 = to_y(after(x1, home)), to_x(after(y2, home))

    far = project(
        [[(d0, None, 0, 1), (d3, None, 3, 1)]],
        frozen_weight, tile_of(frozen_weight.shape[1], 640), after(plan, share[0]), rows, weigh=4, name="far_rows",
    )
    near = project(
        [[(x3, None, 1, 1)], [(y0, None, 1, 1)]],
        frozen_weight, tile, after(plan, home, far), rows, total=near, weigh=4, name="near_rows_rest",
    )
    out = finish(own, near, shrinks[:3], up, plan, 4 * rows)
    return project(
        [[(d1, None, 1, 1), (d2, None, 2, 1)]],
        frozen_weight, tile_of(frozen_weight.shape[1], 640), plan, rows,
        total=far, update=(3, shrinks[3], up), into=out, name="last_rows",
    )


def general(tokens, frozen_weight, down_weight, up_weight, owners, select_slot):
    tp_count = lax.axis_size("tp")
    group = lax.axis_index("grp")
    member = lax.axis_index("tp")
    local_rows, width = tokens.shape
    group_rows = local_rows * tp_count
    blocks_here = group_rows // BLOCK
    rank_columns = down_weight.shape[1]
    column_slice = up_weight.shape[2]
    my_owners = lax.dynamic_slice_in_dim(owners, group * blocks_here, blocks_here)
    arrived_a, arrived_b = (
        lax.all_to_all(
            jnp.take(panels, select_slot, axis=0), "grp", split_axis=0, concat_axis=0, tiled=True
        )
        for panels in (down_weight, up_weight)
    )
    down_tile = jnp.take(arrived_a, my_owners, axis=0)
    up_tile = jnp.take(arrived_b, my_owners, axis=0)
    whole_a = lax.all_gather(down_tile, "tp", axis=2, tiled=True)
    span_rows = min(local_rows, BLOCK)
    pieces_here = local_rows // span_rows
    first_block = member * local_rows // BLOCK
    local_a = lax.dynamic_slice_in_dim(whole_a, first_block, pieces_here, 0)
    shrink_local = jnp.einsum(
        "pnd,prd->pnr",
        tokens.reshape(pieces_here, span_rows, width),
        local_a,
        preferred_element_type=jnp.float32,
    )
    shrink_local = shrink_local.astype(jnp.bfloat16).reshape(local_rows, rank_columns)
    shrink = lax.all_gather(shrink_local, "tp", axis=0, tiled=True)
    frozen_rows = jnp.dot(
        lax.all_gather(tokens, "tp", axis=0, tiled=True),
        frozen_weight,
        preferred_element_type=jnp.float32,
    )
    update_rows = jnp.einsum(
        "bnr,brc->bnc",
        shrink.reshape(blocks_here, BLOCK, rank_columns),
        up_tile,
        preferred_element_type=jnp.float32,
    )
    update_rows = update_rows.reshape(group_rows, column_slice)
    return (frozen_rows + adapter_scale * update_rows).astype(jnp.bfloat16)


def local(tokens, frozen_weight, down_weight, up_weight, adapter_storage_slot, adapter_of_block):
    group_count = lax.axis_size("grp")
    group = lax.axis_index("grp")
    loaded_here = down_weight.shape[0]
    adapters = jnp.arange(adapter_storage_slot.shape[0])
    named = adapter_of_block[:, None] == adapters[None, :]
    slot_numbers = jnp.sum(jnp.where(named, adapter_storage_slot[None, :], 0), axis=1)
    owners = slot_numbers // loaded_here
    offsets = slot_numbers % loaded_here
    owned_here = owners.reshape(group_count, -1) == group
    select_slot = jnp.sum(jnp.where(owned_here, offsets.reshape(group_count, -1), 0), axis=1)
    fits = lax.axis_size("tp") == 4 and tokens.shape[0] == 2 * BLOCK
    way = square if fits else general
    return way(tokens, frozen_weight, down_weight, up_weight, owners, select_slot)


def solution(mesh):
    placed = (
        P(("grp", "tp"), None),
        P(None, "tp"),
        P("grp", None, "tp"),
        P("grp", None, "tp"),
        P(),
        P(),
    )
    return jax.shard_map(
        local, mesh=mesh, in_specs=placed, out_specs=P("grp", "tp"), check_vma=False
    )
```
